256 devices in a mesh: gx: 16 (over z, core), gy: 16 (over y, x).
Axes of the slice: x: 4, y: 4, z: 8, core: 2. Of those that a mesh axis runs over, the one named last changes fastest.
Arguments:
- right_side: float32 [256, 256, 512], P('gx', 'gy'), may hold values from -8 to 8
- coefficient: float32 [256, 256, 512], P('gx', 'gy'), may hold values from 0.5 to 4
Outputs:
- solution: float32 [256, 256, 512], P('gx', 'gy')
The draws below stay inside these ranges and needn't reach their ends.
All inputs are finite; a program needn't handle non-finite values.
Results may differ from the reference program's by a relative error of at most 0.00002.
Values sent between devices are 32-bit elements; how exact they have to be, the bound alone decides.
A program may use at most 128 MiB of HBM per device.

```python
import math
import jax
import jax.numpy as jnp

NZ = 512
LEVELS = 6
DEGREE = 2
COARSE_ITERS = 6
NX = 256
NY = 256


def draw_right_side(key, part):
    key = jax.random.fold_in(key, 7)
    return jnp.clip(2.0 * jax.random.normal(key, (NX, NY, NZ), jnp.float32), -8.0, 8.0)


def levels(own_key, shape, pieces, low, high):
    level, own = 1.0, jax.random.fold_in(own_key, 6)
    for axis_at, parts in pieces:
        heights = jnp.exp(jax.random.uniform(jax.random.fold_in(own, axis_at), (parts,), jnp.float32, low / len(pieces), high / len(pieces)))
        level = level * jnp.repeat(heights, shape[axis_at] // parts).reshape([-1 if axis == axis_at else 1 for axis in range(len(shape))])
    return level


def setup_inputs(seed: int = 0) -> dict:
    seeds = jax.random.split(jax.random.key(seed), 3)
    right_side = draw_right_side(jax.random.fold_in(seeds[2], 71), 0)
    coefficient = jnp.clip(jnp.exp(math.log(4.0) - 2.0794415 * jax.random.uniform(seeds[1], (NX, NY, NZ), jnp.float32) ** levels(seeds[1], (NX, NY, NZ), ((0, 16), (1, 16)), -0.2, 0.2)), 0.5, 4.0)
    return dict(right_side=right_side, coefficient=coefficient)


cheb_centre = 1.15
cheb_radius = 0.85


def pad_vertical(values):
    return jnp.pad(values, ((0, 0), (0, 0), (1, 1)))


def pad_sides(values):
    return jnp.pad(values, ((1, 1), (1, 1), (0, 0)))


def face_weights(padded_coeff):
    center = padded_coeff[1:-1, 1:-1]
    vertical = pad_vertical(center)
    return (0.5 * (center + padded_coeff[:-2, 1:-1]), 0.5 * (center + padded_coeff[2:, 1:-1]),
            0.5 * (center + padded_coeff[1:-1, :-2]), 0.5 * (center + padded_coeff[1:-1, 2:]),
            0.5 * (center + vertical[:, :, :-2]), 0.5 * (center + vertical[:, :, 2:]))


def total_weight(weights):
    return ((((weights[0] + weights[1]) + weights[2]) + weights[3]) + weights[4]) + weights[5]


def apply_operator(values, padded_coeff, halo_fn):
    padded = halo_fn(values)
    vertical = pad_vertical(values)
    weights = face_weights(padded_coeff)
    beside = (weights[0] * padded[:-2, 1:-1] + weights[1] * padded[2:, 1:-1]
              + weights[2] * padded[1:-1, :-2] + weights[3] * padded[1:-1, 2:]
              + weights[4] * vertical[:, :, :-2] + weights[5] * vertical[:, :, 2:])
    return total_weight(weights) * values - beside


def chebyshev(source, initial, steps_count, padded_coeff, inverse_diag, halo_fn):
    rho_previous = cheb_radius / cheb_centre
    if initial is None:
        previous = jnp.zeros_like(source)
        current = inverse_diag * source / cheb_centre
    else:
        previous = initial
        current = initial + inverse_diag * (source - apply_operator(initial, padded_coeff, halo_fn)) / cheb_centre
    for turn_index in range(steps_count - 1):
        rho_current = 1.0 / (2.0 * cheb_centre / cheb_radius - rho_previous)
        update = (current + rho_current * rho_previous * (current - previous)
                  + (2.0 * rho_current / cheb_radius) * inverse_diag
                  * (source - apply_operator(current, padded_coeff, halo_fn)))
        previous, current, rho_previous = current, update, rho_current
    return current


def restrict_sum(values):
    extent = values.shape
    return values.reshape(extent[0] // 2, 2, extent[1] // 2, 2, extent[2] // 2, 2).sum(axis=(1, 3, 5))


def prolong(values):
    return jnp.repeat(jnp.repeat(jnp.repeat(values, 2, 0), 2, 1), 2, 2)


def vcycle_step(source, padded, inverse, halo_fn, lower_solve):
    smoothed = chebyshev(source, None, DEGREE, padded, inverse, halo_fn)
    residual = source - apply_operator(smoothed, padded, halo_fn)
    smoothed = smoothed + prolong(lower_solve(0.5 * restrict_sum(residual)))
    return chebyshev(source, smoothed, DEGREE, padded, inverse, halo_fn)


def level_solve(level_index, source, level_coeff):
    padded = pad_sides(level_coeff)
    inverse = 1.0 / total_weight(face_weights(padded))
    if level_index == LEVELS - 1:
        return chebyshev(source, None, COARSE_ITERS, padded, inverse, pad_sides)
    coarse_coeff = 0.125 * restrict_sum(level_coeff)
    return vcycle_step(source, padded, inverse, pad_sides,
                       lambda coarse_source: level_solve(level_index + 1, coarse_source, coarse_coeff))


def reference(right_side, coefficient):
    return level_solve(0, right_side, coefficient)
```

```python
import functools

import jax
import jax.numpy as jnp
from jax import lax
from jax.experimental import pallas as pl
from jax.experimental.pallas import tpu as pltpu
from jax.sharding import PartitionSpec as P

MESH = pl.DeviceIdType.MESH
F32 = jnp.float32
BF16 = jnp.bfloat16

CENTRE = 1.15
RADIUS = 0.85
COARSE_ITERS = 6
SIGMA = CENTRE / RADIUS
RHO0 = 1.0 / SIGMA
RHO1 = 1.0 / (2.0 * SIGMA - RHO0)
KEEP = 1.0 + RHO1 * RHO0 - 2.0 * RHO1 / RADIUS
OLD = RHO1 * RHO0
STEP = 2.0 * RHO1 / RADIUS
FIRST = 1.0 / CENTRE

NEIGHBOURS = [(dx, dy) for dx in (-1, 0, 1) for dy in (-1, 0, 1) if (dx, dy) != (0, 0)]
ROW0 = 8
LANES = 128


class Fine:
    def __init__(self, parts, n, off, rows, halo_inv):
        self.parts, self.n, self.off, self.rows, self.halo_inv = parts, n, off, rows, halo_inv
        self.planes = n + 2 * off
        self.shape = (parts, self.planes, rows, LANES)

    def tiles(self, halo):
        low, count = ROW0 - halo, self.n + 2 * halo
        if halo == 0:
            return [low + 8 * t for t in range(-(-count // 8))]
        if count % 8 == 0:
            return [low + 8 * t for t in range(count // 8)]
        tiles = -(-count // 8)
        low -= (tiles * 8 - count) // 2
        return [low + 8 * t for t in range(tiles)]


class Coarse:
    def __init__(self, planes, n, step, split):
        self.planes, self.n, self.step, self.split = planes, n, step, split
        self.shape = (planes + 2, n + 16, LANES)
        self.tiles = [ROW0 + 8 * t for t in range(n // 8)]


L0 = Fine(4, 16, 4, 32, 2)
L1 = Fine(2, 8, 6, 24, 4)
L2 = Fine(1, 4, 5, 24, 3)


def roll(value, by):
    return pltpu.roll(value, by % LANES, 1)


def lane_iota():
    return lax.broadcasted_iota(jnp.int32, (8, LANES), 1)


def loop(count, step, fn):
    assert count % step == 0

    def turn(i, carry):
        for k in range(step):
            fn(i * step + k)
        return carry

    lax.fori_loop(0, count // step, turn, 0)


def split3(value):
    high = value.astype(BF16)
    rest = value - high.astype(F32)
    mid = rest.astype(BF16)
    low = (rest - mid.astype(F32)).astype(BF16)
    return high, mid, low


def exact_dot(value, matrix):
    total = None
    for part in split3(value):
        term = jnp.dot(part, matrix, preferred_element_type=F32)
        total = term if total is None else total + term
    return total


def fine_setup(lv, k_ref, w, gx, gy, size_x, size_y):
    wx, wy, wz, inv, diag = w
    h = lv.halo_inv
    lane = lane_iota()
    row = lax.broadcasted_iota(jnp.int32, (8, LANES), 0)
    parts = lv.parts

    def plane(i):
        x = lv.off - h + i
        gx_cell = gx * lv.n + (i - h)
        in_x = jnp.logical_and(gx_cell >= 0, gx_cell < size_x)
        for r in lv.tiles(h):
            cells = [k_ref[p, x, pl.ds(r, 8), :] for p in range(parts)]
            gy_cell = gy * lv.n + (r - ROW0) + row
            inside = jnp.logical_and(jnp.logical_and(gy_cell >= 0, gy_cell < size_y), in_x)
            first = jnp.where(lane == 0, 0.0, roll(cells[parts - 1], 1))
            last = jnp.where(lane == LANES - 1, 0.0, roll(cells[0], -1))
            for p in range(parts):
                k = cells[p]
                kxm = k_ref[p, x - 1, pl.ds(r, 8), :]
                kxp = k_ref[p, x + 1, pl.ds(r, 8), :]
                kym = k_ref[p, x, pl.ds(r - 1, 8), :]
                kyp = k_ref[p, x, pl.ds(r + 1, 8), :]
                kzm = first if p == 0 else cells[p - 1]
                kzp = last if p == parts - 1 else cells[p + 1]
                wx[p, x, pl.ds(r, 8), :] = 0.5 * (k + kxm)
                wy[p, x, pl.ds(r, 8), :] = 0.5 * (k + kym)
                down = 0.5 * (k + kzm)
                if p == 0:
                    down = jnp.where(lane == 0, 0.0, down)
                    wz[parts, x, pl.ds(r, 8), :] = roll(down, -1)
                wz[p, x, pl.ds(r, 8), :] = down
                d = 3.0 * k + 0.5 * (((kxm + kxp) + (kym + kyp)) + (kzm + kzp))
                diag[p, x, pl.ds(r, 8), :] = d
                inv[p, x, pl.ds(r, 8), :] = jnp.where(inside, 1.0 / d, 0.0)

    count = lv.n + 2 * h + 1
    loop(count, 1, plane)


def fine_sum(lv, v_ref, w, x, r):
    wx, wy, wz = w[0], w[1], w[2]
    parts = lv.parts
    cells = [v_ref[p, x, pl.ds(r, 8), :] for p in range(parts)]
    below, above = roll(cells[parts - 1], 1), roll(cells[0], -1)
    sums = []
    for p in range(parts):
        along_x = (
            wx[p, x, pl.ds(r, 8), :] * v_ref[p, x - 1, pl.ds(r, 8), :]
            + wx[p, x + 1, pl.ds(r, 8), :] * v_ref[p, x + 1, pl.ds(r, 8), :]
        )
        along_y = (
            wy[p, x, pl.ds(r, 8), :] * v_ref[p, x, pl.ds(r - 1, 8), :]
            + wy[p, x, pl.ds(r + 1, 8), :] * v_ref[p, x, pl.ds(r + 1, 8), :]
        )
        along_z = wz[p, x, pl.ds(r, 8), :] * (below if p == 0 else cells[p - 1]) + wz[
            p + 1, x, pl.ds(r, 8), :
        ] * (above if p == parts - 1 else cells[p + 1])
        sums.append((along_x + along_y) + along_z)
    return sums, cells


def fine_first(lv, b_ref, w, out_ref, halo):
    inv = w[3]

    def plane(i):
        x = lv.off - halo + i
        for r in lv.tiles(halo):
            for p in range(lv.parts):
                at = (p, x, pl.ds(r, 8), slice(None))
                out_ref[at] = FIRST * (inv[at] * b_ref[at])

    loop(lv.n + 2 * halo, 2, plane)


def fine_step(lv, b_ref, w, v_ref, old_ref, out_ref, halo, keep, old, step):
    inv = w[3]

    def plane(i):
        x = lv.off - halo + i
        for r in lv.tiles(halo):
            sums, cells = fine_sum(lv, v_ref, w, x, r)
            for p in range(lv.parts):
                at = (p, x, pl.ds(r, 8), slice(None))
                value = keep * cells[p] + step * (inv[at] * (b_ref[at] + sums[p]))
                if old_ref is not None:
                    value = value - old * old_ref[at]
                out_ref[at] = value

    loop(lv.n + 2 * halo, 2, plane)


def fine_restrict(lv, b_ref, w, v_ref, tmp_ref):
    diag = w[4]
    parts = lv.parts

    def pair(i):
        for r in lv.tiles(0):
            total = [None] * max(parts // 2, 1)
            for k in range(2):
                x = lv.off + 2 * i + k
                sums, cells = fine_sum(lv, v_ref, w, x, r)
                for p in range(parts):
                    at = (p, x, pl.ds(r, 8), slice(None))
                    res = (b_ref[at] + sums[p]) - diag[at] * cells[p]
                    q = p // 2
                    total[q] = res if total[q] is None else total[q] + res
            for q, value in enumerate(total):
                tmp_ref[q, i, pl.ds(r - ROW0, 8), :] = value

    loop(lv.n // 2, 1, pair)


def fold_x(lv, k_ref, tmp_ref):
    def pair(i):
        for r in lv.tiles(0):
            for q in range(max(lv.parts // 2, 1)):
                total = None
                for p in range(lv.parts):
                    if p // 2 == q:
                        for k in range(2):
                            value = k_ref[p, lv.off + 2 * i + k, pl.ds(r, 8), :]
                            total = value if total is None else total + value
                tmp_ref[q, i, pl.ds(r - ROW0, 8), :] = total

    loop(lv.n // 2, 1, pair)


def fold_y(lv, tmp_ref, out_ref, off, scale):
    half = lv.n // 2
    for q in range(lv.parts // 2):
        for i in range(half):
            even = tmp_ref[q, i, pl.ds(0, half, stride=2), :]
            odd = tmp_ref[q, i, pl.ds(1, half, stride=2), :]
            out_ref[q, off + i, pl.ds(ROW0, half), :] = scale * (even + odd)


def fold_z(tmp_ref, left_ref, matrix, scale):
    for i in range(2):
        for j in range(2):
            row = tmp_ref[0, i, pl.ds(2 * j, 1), :] + tmp_ref[0, i, pl.ds(2 * j + 1, 1), :]
            left_ref[pl.ds(i, 1), pl.ds(LANES * j, LANES)] = scale * row
    return exact_dot(left_ref[...], matrix)


def fine_correct(lv, next_lv, e_ref, s_ref, t_ref, halo):
    next_halo = -(-halo // 2)
    row_lo = ROW0 - next_halo
    rows = next_lv.n + 2 * next_halo
    starts = [row_lo + 8 * t for t in range(-(-rows // 8))]
    if len(starts) == 2:
        starts = [4, 12]

    def plane(i):
        big = next_lv.off - next_halo + i
        for q in range(next_lv.parts):
            for r in starts:
                e = e_ref[q, big, pl.ds(r, 8), :]
                base = 2 * (r - ROW0) + ROW0
                for p in (2 * q, 2 * q + 1):
                    for k in range(2):
                        x = lv.off + 2 * (i - next_halo) + k
                        for c in range(2):
                            at = (p, x, pl.ds(base + c, 8, stride=2), slice(None))
                            t_ref[at] = s_ref[at] + e

    loop(next_lv.n + 2 * next_halo, 1, plane)


def coarse_rolls(lv, ref, first, count, r):
    return [roll(ref[first - 1 + i, pl.ds(r, 8), :], LANES // 2) for i in range(count + 2)]


def coarse_beside(lv, ref, first, count, r):
    out = []
    low = lane_iota() < LANES // 2
    turned = coarse_rolls(lv, ref, first, count, r) if lv.split else None
    for i in range(count):
        y = first + i
        v = ref[y, pl.ds(r, 8), :]
        xm, xp = ref[y, pl.ds(r - 1, 8), :], ref[y, pl.ds(r + 1, 8), :]
        if lv.split:
            ym = jnp.where(low, turned[i], turned[i + 1])
            yp = jnp.where(low, turned[i + 1], turned[i + 2])
        else:
            ym, yp = ref[y - 1, pl.ds(r, 8), :], ref[y + 1, pl.ds(r, 8), :]
        out.append((v, xm, xp, ym, yp, roll(v, lv.step), roll(v, -lv.step)))
    return out


def coarse_setup(lv, k_ref, w):
    lane = lane_iota() % (LANES // 2)
    bottom, top = lane < lv.step, lane >= LANES // 2 - lv.step
    group = 2

    def planes(i):
        first = 1 + group * i
        for r in lv.tiles:
            for j, (k, xm, xp, ym, yp, zm, zp) in enumerate(
                coarse_beside(lv, k_ref, first, group, r)
            ):
                y = first + j
                zm, zp = jnp.where(bottom, 0.0, zm), jnp.where(top, 0.0, zp)
                w[0][0, y, pl.ds(r, 8), :] = 0.5 * (k + xm)
                w[0][1, y, pl.ds(r, 8), :] = 0.5 * (k + xp)
                w[0][2, y, pl.ds(r, 8), :] = 0.5 * (k + ym)
                w[0][3, y, pl.ds(r, 8), :] = 0.5 * (k + yp)
                w[0][4, y, pl.ds(r, 8), :] = jnp.where(bottom, 0.0, 0.5 * (k + zm))
                w[0][5, y, pl.ds(r, 8), :] = jnp.where(top, 0.0, 0.5 * (k + zp))
                d = 3.0 * k + 0.5 * (((xm + xp) + (ym + yp)) + (zm + zp))
                w[0][6, y, pl.ds(r, 8), :] = d
                w[0][7, y, pl.ds(r, 8), :] = 1.0 / d

    loop(lv.planes // group, 1, planes)


def coarse_apply(lv, w, v_ref, fn, group=4):
    def planes(i):
        first = 1 + group * i
        for r in lv.tiles:
            for j, beside in enumerate(coarse_beside(lv, v_ref, first, group, r)):
                y = first + j
                total = None
                for f in range(6):
                    term = w[0][f, y, pl.ds(r, 8), :] * beside[1 + f]
                    total = term if total is None else total + term
                fn(y, r, beside[0], total)

    loop(lv.planes // group, 1, planes)


def coarse_first(lv, b_ref, w, out_ref):
    def plane(i):
        for r in lv.tiles:
            at = (1 + i, pl.ds(r, 8), slice(None))
            out_ref[at] = FIRST * (w[0][7, 1 + i, pl.ds(r, 8), :] * b_ref[at])

    loop(lv.planes, 4, plane)


def coarse_step(lv, b_ref, w, v_ref, old_ref, out_ref, keep, old, step):
    def tile(y, r, v, total):
        at = (y, pl.ds(r, 8), slice(None))
        value = keep * v + step * (w[0][7, y, pl.ds(r, 8), :] * (b_ref[at] + total))
        if old_ref is not None:
            value = value - old * old_ref[at]
        out_ref[at] = value

    coarse_apply(lv, w, v_ref, tile)


def coarse_residual(lv, b_ref, w, v_ref, out_ref):
    def tile(y, r, v, total):
        at = (y, pl.ds(r, 8), slice(None))
        out_ref[at] = (b_ref[at] + total) - w[0][6, y, pl.ds(r, 8), :] * v

    coarse_apply(lv, w, v_ref, tile)


def coarse_fold(lv, next_lv, ref, out_ref, scale):
    lane = lane_iota()
    even = (lane // lv.step) % 2 == 0
    joined = lv.planes // next_lv.planes

    def plane(i):
        for r in next_lv.tiles:
            base = ROW0 + 2 * (r - ROW0)
            total = None
            for j in range(joined):
                for c in range(2):
                    value = ref[1 + joined * i + j, pl.ds(base + c, 8, stride=2), :]
                    total = value if total is None else total + value
            if lv.split:
                total = total + roll(total, LANES // 2)
            other = jnp.where(even, roll(total, -lv.step), roll(total, lv.step))
            out_ref[1 + i, pl.ds(r, 8), :] = scale * (total + other)

    loop(next_lv.planes, 4, plane)


def coarse_correct(lv, next_lv, e_ref, s_ref, t_ref):
    joined = lv.planes // next_lv.planes

    def plane(i):
        for r in next_lv.tiles:
            e = e_ref[1 + i, pl.ds(r, 8), :]
            base = ROW0 + 2 * (r - ROW0)
            for j in range(joined):
                for c in range(2):
                    at = (1 + joined * i + j, pl.ds(base + c, 8, stride=2), slice(None))
                    t_ref[at] = s_ref[at] + e

    loop(next_lv.planes, 4, plane)


def zero_margin(lv, ref):
    zero = jnp.zeros((8, LANES), F32)
    for y in (0, lv.planes + 1):
        for r in lv.tiles:
            ref[y, pl.ds(r, 8), :] = zero

    def plane(y):
        ref[y, pl.ds(0, 8), :] = zero
        ref[y, pl.ds(ROW0 + lv.n, 8), :] = zero

    loop(lv.planes + 2, 1, plane)


class Links:
    def __init__(self, send, recv):
        self.send, self.recv, self.used = send, recv, 0

    def copy(self, src, dst, device):
        index = self.used
        self.used += 1
        return pltpu.make_async_remote_copy(
            src_ref=src,
            dst_ref=dst,
            send_sem=self.send.at[index],
            recv_sem=self.recv.at[index],
            device_id=device,
            device_id_type=MESH,
        )


class Halo:
    def __init__(self, place, links, sources, targets):
        self.place = place
        gx, gy = place[0], place[1]
        self.copies = [
            (d, links.copy(sources[d], targets[d], (gx + d[0], gy + d[1]))) for d in NEIGHBOURS
        ]

    def start(self):
        for (dx, dy), copy in self.copies:
            pl.when(there(self.place, dx, dy))(copy.start)

    def wait_recv(self):
        for (dx, dy), copy in self.copies:
            pl.when(there(self.place, -dx, -dy))(copy.wait_recv)

    def wait_send(self):
        for (dx, dy), copy in self.copies:
            pl.when(there(self.place, dx, dy))(copy.wait_send)


def there(place, dx, dy):
    gx, gy, nx, ny = place
    ok = None
    for at, by, size in ((gx, dx, nx), (gy, dy, ny)):
        if by:
            test = at + by < size if by > 0 else at + by >= 0
            ok = test if ok is None else jnp.logical_and(ok, test)
    return True if ok is None else ok


class Rim:
    def __init__(self, lv, halo, refs):
        self.lv, self.halo = lv, halo
        self.send_x, self.send_y, self.recv_x, self.recv_y = refs

    @staticmethod
    def scratch(lv, halo):
        n, parts = lv.n, lv.parts
        return [
            pltpu.VMEM((2, parts, halo, n, LANES), F32),
            pltpu.VMEM((2, parts, n, halo, LANES), F32),
            pltpu.VMEM((2, parts, halo, n, LANES), F32),
            pltpu.VMEM((2, parts, n + 2 * halo, halo, LANES), F32),
        ]

    def pack(self, ref):
        lv, h = self.lv, self.halo
        for side, start in ((0, lv.off), (1, lv.off + lv.n - h)):
            for p in range(lv.parts):
                for i in range(h):
                    self.send_x[side, p, i] = ref[p, start + i, pl.ds(ROW0, lv.n), :]

        def plane(i):
            for p in range(lv.parts):
                self.send_y[0, p, i] = ref[p, lv.off + i, pl.ds(ROW0, h), :]
                self.send_y[1, p, i] = ref[p, lv.off + i, pl.ds(ROW0 + lv.n - h, h), :]

        loop(lv.n, 2, plane)

    def exchange(self, place, links):
        lv, h, n = self.lv, self.halo, self.lv.n
        sources, targets = {}, {}
        for dx, dy in NEIGHBOURS:
            if dy == 0:
                sources[dx, dy] = self.send_x.at[1 if dx > 0 else 0]
                targets[dx, dy] = self.recv_x.at[0 if dx > 0 else 1]
            else:
                src = self.send_y.at[1 if dy > 0 else 0]
                dst = self.recv_y.at[0 if dy > 0 else 1]
                if dx == 0:
                    sources[dx, dy] = src
                    targets[dx, dy] = dst.at[:, h : h + n]
                elif dx > 0:
                    sources[dx, dy] = src.at[:, n - h : n]
                    targets[dx, dy] = dst.at[:, 0:h]
                else:
                    sources[dx, dy] = src.at[:, 0:h]
                    targets[dx, dy] = dst.at[:, h + n : n + 2 * h]
        return Halo(place, links, sources, targets)

    def unpack(self, ref, place):
        lv, h, n = self.lv, self.halo, self.lv.n
        for side, start, dx in ((0, lv.off - h, -1), (1, lv.off + n, 1)):
            ok = there(place, dx, 0)
            for p in range(lv.parts):
                for i in range(h):
                    value = self.recv_x[side, p, i]
                    ref[p, start + i, pl.ds(ROW0, n), :] = jnp.where(ok, value, 0.0)

        gx, gy, nx, ny = place

        def plane(i):
            cell = gx * n + (i - h)
            in_x = jnp.logical_and(cell >= 0, cell < nx * n)
            for side, row, dy in ((0, ROW0 - h, -1), (1, ROW0 + n, 1)):
                ok = jnp.logical_and(in_x, there(place, 0, dy))
                for p in range(lv.parts):
                    value = self.recv_y[side, p, i]
                    ref[p, lv.off - h + i, pl.ds(row, h), :] = jnp.where(ok, value, 0.0)

        loop(n + 2 * h, 2, plane)


class Blocks:
    def __init__(self, lv, refs):
        self.lv = lv
        self.send, self.recv = refs

    @staticmethod
    def scratch(lv):
        n = lv.n
        return [pltpu.VMEM((n, n, LANES), F32), pltpu.VMEM((3, 3 * n, n, LANES), F32)]

    def pack(self, ref):
        lv = self.lv
        for i in range(lv.n):
            self.send[i] = ref[0, lv.off + i, pl.ds(ROW0, lv.n), :]

    def exchange(self, place, links):
        n = self.lv.n
        sources = {d: self.send for d in NEIGHBOURS}
        targets = {
            (dx, dy): self.recv.at[1 - dy, n * (1 - dx) : n * (1 - dx) + n] for dx, dy in NEIGHBOURS
        }
        return Halo(place, links, sources, targets)

    def unpack(self, ref, place):
        lv, n = self.lv, self.lv.n
        for j in range(3):
            for i in range(3):
                if (i, j) == (1, 1):
                    continue
                ok = there(place, i - 1, j - 1)
                for k in range(n):
                    value = self.recv[j, n * i + k]
                    ref[0, lv.off + n * (i - 1) + k, pl.ds(ROW0 + n * (j - 1), n), :] = jnp.where(
                        ok, value, 0.0
                    )


class Gather:
    def __init__(self, place, links, piece_ref, whole_ref):
        gx, gy, nx, ny = place
        self.place = place
        self.piece, self.whole = piece_ref, whole_ref
        mine = piece_ref.at[gx]
        self.along_x = [
            links.copy(mine, mine, (lax.rem(gx + d, nx), gy)) for d in range(1, nx)
        ]
        slab = whole_ref.at[1 + gy, pl.ds(ROW0, 2 * nx), :]
        self.along_y = [
            links.copy(slab, slab, (gx, lax.rem(gy + d, ny))) for d in range(1, ny)
        ]

    def start_x(self, value):
        gx = self.place[0]
        self.piece[gx] = value
        for copy in self.along_x:
            copy.start()

    def start_y(self):
        gx, gy, nx, ny = self.place
        for copy in self.along_x:
            copy.wait_recv()
        for i in range(nx):
            self.whole[1 + gy, pl.ds(ROW0 + 2 * i, 2), :] = self.piece[i]
        for copy in self.along_y:
            copy.start()

    def finish(self):
        for copy in self.along_y:
            copy.wait_recv()

    def wait_send(self):
        for copy in self.along_x + self.along_y:
            copy.wait_send()


def scratch_shapes(nx, ny):
    l3, l4, l5 = coarse_levels(nx, ny)
    shapes = {}
    for name in ("raw_k", "raw_b", "out"):
        shapes[name] = pltpu.VMEM((L0.n, L0.n, L0.parts * LANES), F32)
    shapes["perm"] = pltpu.VMEM((512, 512), BF16)
    shapes["back"] = pltpu.VMEM((512, 512), BF16)
    shapes["left"] = pltpu.VMEM((8, 2 * LANES), F32)
    for i, lv in enumerate((L0, L1, L2)):
        for name in ("k", "b", "wx", "wy", "inv", "diag", "x", "s", "t"):
            shapes[name + str(i)] = pltpu.VMEM(lv.shape, F32)
        shapes["wz" + str(i)] = pltpu.VMEM((lv.parts + 1,) + lv.shape[1:], F32)
        shapes["tmp" + str(i)] = pltpu.VMEM((max(lv.parts // 2, 1), lv.n // 2, max(lv.n, 8), LANES), F32)
    shapes["e2"] = pltpu.VMEM((6, L2.rows, LANES), F32)
    for i, lv in ((3, l3), (4, l4), (5, l5)):
        for name in ("k", "b", "x", "s", "t"):
            shapes[name + str(i)] = pltpu.VMEM(lv.shape, F32)
        shapes["w" + str(i)] = pltpu.VMEM((8,) + lv.shape, F32)
    for name, lv, halo in (("rk0", L0, 3), ("rb0", L0, 2), ("rs0", L0, 2), ("rk1", L1, 5), ("rb1", L1, 4)):
        for j, shape in enumerate(Rim.scratch(lv, halo)):
            shapes[name + "_" + str(j)] = shape
    for name in ("rk2", "rb2", "rs2"):
        for j, shape in enumerate(Blocks.scratch(L2)):
            shapes[name + "_" + str(j)] = shape
    for name in ("pk3", "pb3"):
        shapes[name] = pltpu.VMEM((nx, 2, LANES), F32)
    copies = 8 * 8 + 2 * (nx - 1 + ny - 1)
    shapes["send"] = pltpu.SemaphoreType.DMA((copies,))
    shapes["recv"] = pltpu.SemaphoreType.DMA((copies,))
    shapes["local"] = pltpu.SemaphoreType.DMA((3,))
    return shapes


def coarse_levels(nx, ny):
    return (
        Coarse(ny, 2 * nx, 1, True),
        Coarse(ny, nx, 2, False),
        Coarse(ny // 2, nx // 2, 4, False),
    )


def kernel(nx, ny, names, b_in, k_in, out_ref, *refs):
    m = dict(zip(names, refs))
    gx, gy = lax.axis_index("gx"), lax.axis_index("gy")
    place = (gx, gy, nx, ny)
    l3, l4, l5 = coarse_levels(nx, ny)
    links = Links(m["send"], m["recv"])

    def pair(name, cls, *args):
        refs = [m[key] for key in names if key.startswith(name + "_")]
        return cls(*args, refs)

    rk0, rb0, rs0 = (pair(name, Rim, L0, h) for name, h in (("rk0", 3), ("rb0", 2), ("rs0", 2)))
    rk1, rb1 = (pair(name, Rim, L1, h) for name, h in (("rk1", 5), ("rb1", 4)))
    rk2, rb2, rs2 = (pair(name, Blocks, L2) for name in ("rk2", "rb2", "rs2"))
    hk0, hb0, hs0, hk1, hb1, hk2, hb2, hs2 = (
        rim.exchange(place, links) for rim in (rk0, rb0, rs0, rk1, rb1, rk2, rb2, rs2)
    )
    gk3 = Gather(place, links, m["pk3"], m["k3"])
    gb3 = Gather(place, links, m["pb3"], m["b3"])

    load_k = pltpu.make_async_copy(k_in, m["raw_k"], m["local"].at[0])
    load_b = pltpu.make_async_copy(b_in, m["raw_b"], m["local"].at[1])
    load_k.start()
    load_b.start()

    barrier = pltpu.get_barrier_semaphore()
    for d in range(1, nx):
        pl.semaphore_signal(
            barrier, inc=1, device_id=(lax.rem(gx + d, nx), gy), device_id_type=MESH
        )
    for d in range(1, ny):
        pl.semaphore_signal(
            barrier, inc=1, device_id=(gx, lax.rem(gy + d, ny)), device_id_type=MESH
        )
    corners = [d for d in NEIGHBOURS if d[0] and d[1]]
    for dx, dy in corners:

        @pl.when(there(place, dx, dy))
        def _():
            pl.semaphore_signal(
                barrier, inc=1, device_id=(gx + dx, gy + dy), device_id_type=MESH
            )

    def one(rows, cols, test):
        at = lax.broadcasted_iota(jnp.int32, (rows, cols), 0)
        to = lax.broadcasted_iota(jnp.int32, (rows, cols), 1)
        return jnp.where(test(at, to), 1.0, 0.0).astype(BF16)

    def fill(i):
        start = pl.multiple_of(i * 64, 64)
        m["perm"][pl.ds(start, 64), :] = one(
            64, 512, lambda at, to: at + start == 4 * (to % LANES) + to // LANES
        )
        m["back"][pl.ds(start, 64), :] = one(
            64, 512, lambda at, to: to == 4 * ((at + start) % LANES) + (at + start) // LANES
        )

    loop(8, 1, fill)
    m["left"][...] = jnp.zeros_like(m["left"])
    fold = one(
        2 * LANES,
        LANES,
        lambda at, to: jnp.logical_and(at // LANES == to // 64, (at % LANES) // 2 == to % 64),
    )
    unfold = one(
        LANES,
        2 * LANES,
        lambda at, to: jnp.logical_and(to // LANES == at // 64, (to % LANES) // 2 == at % 64),
    )

    def reorder(raw, ref):
        half = L0.n // 2
        for c in range(2):
            value = raw[c * half : (c + 1) * half].reshape(half * L0.n, 512)
            moved = exact_dot(value, m["perm"][...])
            for p in range(L0.parts):
                ref[p, pl.ds(L0.off + c * half, half), pl.ds(ROW0, L0.n), :] = moved[
                    :, p * LANES : (p + 1) * LANES
                ].reshape(half, L0.n, LANES)

    load_k.wait()
    reorder(m["raw_k"], m["k0"])
    rk0.pack(m["k0"])
    beside_x = jnp.where(gx > 0, 1, 0) + jnp.where(gx < nx - 1, 1, 0)
    beside_y = jnp.where(gy > 0, 1, 0) + jnp.where(gy < ny - 1, 1, 0)
    pl.semaphore_wait(barrier, nx - 1 + ny - 1 + beside_x * beside_y)
    hk0.start()
    load_b.wait()
    reorder(m["raw_b"], m["b0"])
    rb0.pack(m["b0"])
    hb0.start()

    fold_x(L0, m["k0"], m["tmp0"])
    fold_y(L0, m["tmp0"], m["k1"], L1.off, 0.125)
    rk1.pack(m["k1"])
    hk1.start()
    fold_x(L1, m["k1"], m["tmp1"])
    fold_y(L1, m["tmp1"], m["k2"], L2.off, 0.125)
    rk2.pack(m["k2"])
    hk2.start()
    fold_x(L2, m["k2"], m["tmp2"])
    gk3.start_x(fold_z(m["tmp2"], m["left"], fold, 0.125)[0:2])
    for lv, i in ((l3, 3), (l4, 4), (l5, 5)):
        for name in ("k", "x", "s", "t"):
            zero_margin(lv, m[name + str(i)])

    weights = [
        tuple(m[name + str(i)] for name in ("wx", "wy", "wz", "inv", "diag")) for i in range(3)
    ]
    sizes = [(nx * lv.n, ny * lv.n) for lv in (L0, L1, L2)]
    w3, w4, w5 = (m["w3"],), (m["w4"],), (m["w5"],)

    hk0.wait_recv()
    rk0.unpack(m["k0"], place)
    fine_setup(L0, m["k0"], weights[0], gx, gy, *sizes[0])
    hb0.wait_recv()
    rb0.unpack(m["b0"], place)
    fine_first(L0, m["b0"], weights[0], m["x0"], 2)
    fine_step(L0, m["b0"], weights[0], m["x0"], None, m["s0"], 1, KEEP, OLD, STEP)
    fine_restrict(L0, m["b0"], weights[0], m["s0"], m["tmp0"])
    fold_y(L0, m["tmp0"], m["b1"], L1.off, 0.5)
    rb1.pack(m["b1"])
    hb1.start()
    rs0.pack(m["s0"])
    hs0.start()

    gk3.start_y()
    hk1.wait_recv()
    rk1.unpack(m["k1"], place)
    fine_setup(L1, m["k1"], weights[1], gx, gy, *sizes[1])
    hb1.wait_recv()
    rb1.unpack(m["b1"], place)
    fine_first(L1, m["b1"], weights[1], m["x1"], 4)
    fine_step(L1, m["b1"], weights[1], m["x1"], None, m["s1"], 3, KEEP, OLD, STEP)
    fine_restrict(L1, m["b1"], weights[1], m["s1"], m["tmp1"])
    fold_y(L1, m["tmp1"], m["b2"], L2.off, 0.5)
    rb2.pack(m["b2"])
    hb2.start()

    hk2.wait_recv()
    rk2.unpack(m["k2"], place)
    fine_setup(L2, m["k2"], weights[2], gx, gy, *sizes[2])
    hb2.wait_recv()
    rb2.unpack(m["b2"], place)
    fine_first(L2, m["b2"], weights[2], m["x2"], 2)
    fine_step(L2, m["b2"], weights[2], m["x2"], None, m["s2"], 1, KEEP, OLD, STEP)
    fine_restrict(L2, m["b2"], weights[2], m["s2"], m["tmp2"])
    gb3.start_x(fold_z(m["tmp2"], m["left"], fold, 0.5)[0:2])
    rs2.pack(m["s2"])
    hs2.start()

    gk3.finish()
    coarse_setup(l3, m["k3"], w3)
    gb3.start_y()
    coarse_fold(l3, l4, m["k3"], m["k4"], 0.125)
    coarse_setup(l4, m["k4"], w4)
    coarse_fold(l4, l5, m["k4"], m["k5"], 0.125)
    coarse_setup(l5, m["k5"], w5)
    gb3.finish()

    coarse_first(l3, m["b3"], w3, m["x3"])
    coarse_step(l3, m["b3"], w3, m["x3"], None, m["s3"], KEEP, OLD, STEP)
    coarse_residual(l3, m["b3"], w3, m["s3"], m["t3"])
    coarse_fold(l3, l4, m["t3"], m["b4"], 0.5)
    coarse_first(l4, m["b4"], w4, m["x4"])
    coarse_step(l4, m["b4"], w4, m["x4"], None, m["s4"], KEEP, OLD, STEP)
    coarse_residual(l4, m["b4"], w4, m["s4"], m["t4"])
    coarse_fold(l4, l5, m["t4"], m["b5"], 0.5)
    coarse_first(l5, m["b5"], w5, m["x5"])
    now, old, spare = m["x5"], None, [m["s5"], m["t5"]]
    rho = RHO0
    for _ in range(COARSE_ITERS - 1):
        rho_new = 1.0 / (2.0 * SIGMA - rho)
        keep = 1.0 + rho_new * rho - 2.0 * rho_new / RADIUS
        out = spare.pop(0)
        coarse_step(l5, m["b5"], w5, now, old, out, keep, rho_new * rho, 2.0 * rho_new / RADIUS)
        if old is not None:
            spare.append(old)
        now, old, rho = out, now, rho_new
    coarse_correct(l4, l5, now, m["s4"], m["t4"])
    coarse_step(l4, m["b4"], w4, m["t4"], None, m["x4"], 1.0 - FIRST, 0.0, FIRST)
    coarse_step(l4, m["b4"], w4, m["x4"], m["t4"], m["s4"], KEEP, OLD, STEP)
    coarse_correct(l3, l4, m["s4"], m["s3"], m["t3"])
    coarse_step(l3, m["b3"], w3, m["t3"], None, m["x3"], 1.0 - FIRST, 0.0, FIRST)
    coarse_step(l3, m["b3"], w3, m["x3"], m["t3"], m["s3"], KEEP, OLD, STEP)

    near = jnp.concatenate(
        [m["s3"][gy + d, pl.ds(2 * gx + ROW0 - 2, 8), :] for d in range(3)], axis=0
    )
    wide = exact_dot(near, unfold)
    for d in range(3):
        for i in range(6):
            for a in range(2):
                row = wide[8 * d + i : 8 * d + i + 1, a * LANES : (a + 1) * LANES]
                m["e2"][i, pl.ds(ROW0 - 4 + 4 * d + 2 * a, 2), :] = jnp.broadcast_to(
                    row, (2, LANES)
                )
    hs2.wait_recv()
    hs2.wait_send()
    rs2.unpack(m["s2"], place)
    for i in range(6):
        for k in range(2):
            x = L2.off - 4 + 2 * i + k
            for r in L2.tiles(4):
                m["t2"][0, x, pl.ds(r, 8), :] = (
                    m["s2"][0, x, pl.ds(r, 8), :] + m["e2"][i, pl.ds(r, 8), :]
                )
    fine_step(L2, m["b2"], weights[2], m["t2"], None, m["x2"], 3, 1.0 - FIRST, 0.0, FIRST)
    fine_step(L2, m["b2"], weights[2], m["x2"], m["t2"], m["s2"], 2, KEEP, OLD, STEP)

    fine_correct(L1, L2, m["s2"], m["s1"], m["t1"], 3)
    fine_step(L1, m["b1"], weights[1], m["t1"], None, m["x1"], 2, 1.0 - FIRST, 0.0, FIRST)
    fine_step(L1, m["b1"], weights[1], m["x1"], m["t1"], m["s1"], 1, KEEP, OLD, STEP)

    hs0.wait_recv()
    hs0.wait_send()
    rs0.unpack(m["s0"], place)
    fine_correct(L0, L1, m["s1"], m["s0"], m["t0"], 2)
    fine_step(L0, m["b0"], weights[0], m["t0"], None, m["x0"], 1, 1.0 - FIRST, 0.0, FIRST)
    fine_step(L0, m["b0"], weights[0], m["x0"], m["t0"], m["s0"], 0, KEEP, OLD, STEP)

    half = L0.n // 2
    for c in range(2):
        value = jnp.concatenate(
            [
                m["s0"][p, pl.ds(L0.off + c * half, half), pl.ds(ROW0, L0.n), :].reshape(
                    half * L0.n, LANES
                )
                for p in range(L0.parts)
            ],
            axis=1,
        )
        moved = exact_dot(value, m["back"][...])
        m["out"][c * half : (c + 1) * half] = moved.reshape(half, L0.n, 512)
    store = pltpu.make_async_copy(m["out"], out_ref, m["local"].at[2])
    store.start()
    for part in (hk0, hb0, hk1, hb1, hk2, hb2, gk3, gb3):
        part.wait_send()
    store.wait()


def solution(mesh):
    nx, ny = mesh.shape["gx"], mesh.shape["gy"]
    shapes = scratch_shapes(nx, ny)

    def body(right_side, coefficient):
        return pl.pallas_call(
            functools.partial(kernel, nx, ny, list(shapes)),
            out_shape=jax.ShapeDtypeStruct(right_side.shape, F32),
            in_specs=[pl.BlockSpec(memory_space=pl.ANY)] * 2,
            out_specs=pl.BlockSpec(memory_space=pl.ANY),
            scratch_shapes=list(shapes.values()),
            compiler_params=pltpu.CompilerParams(
                collective_id=0, has_side_effects=True, vmem_limit_bytes=56 * 1024 * 1024
            ),
        )(right_side, coefficient)

    return jax.shard_map(
        body,
        mesh=mesh,
        in_specs=(P("gx", "gy", None), P("gx", "gy", None)),
        out_specs=P("gx", "gy", None),
        check_vma=False,
    )
```

```python
import functools

import jax
import jax.numpy as jnp
from jax import lax
from jax.experimental import pallas as pl
from jax.experimental.pallas import tpu as pltpu
from jax.sharding import PartitionSpec as P

MESH = pl.DeviceIdType.MESH
F32 = jnp.float32
BF16 = jnp.bfloat16

CENTRE = 1.15
RADIUS = 0.85
COARSE_ITERS = 6
SIGMA = CENTRE / RADIUS
RHO0 = 1.0 / SIGMA
RHO1 = 1.0 / (2.0 * SIGMA - RHO0)
KEEP = 1.0 + RHO1 * RHO0 - 2.0 * RHO1 / RADIUS
OLD = RHO1 * RHO0
STEP = 2.0 * RHO1 / RADIUS
FIRST = 1.0 / CENTRE

NEIGHBOURS = [(dx, dy) for dx in (-1, 0, 1) for dy in (-1, 0, 1) if (dx, dy) != (0, 0)]
ROW0 = 8
LANES = 128


class Fine:
    def __init__(self, parts, n, off, rows, halo_inv):
        self.parts, self.n, self.off, self.rows, self.halo_inv = parts, n, off, rows, halo_inv
        self.planes = n + 2 * off
        self.shape = (parts, self.planes, rows, LANES)

    def tiles(self, halo):
        low, count = ROW0 - halo, self.n + 2 * halo
        if halo == 0:
            return [low + 8 * t for t in range(-(-count // 8))]
        if count % 8 == 0:
            return [low + 8 * t for t in range(count // 8)]
        tiles = -(-count // 8)
        low = max(1, low - (tiles * 8 - count) // 2)
        return [low + 8 * t for t in range(tiles)]


class Coarse:
    def __init__(self, planes, n, step, split):
        self.planes, self.n, self.step, self.split = planes, n, step, split
        self.shape = (planes + 2, n + 16, LANES)
        self.tiles = [ROW0 + 8 * t for t in range(n // 8)]


L0 = Fine(4, 16, 4, 32, 2)
L1 = Fine(2, 8, 8, 32, 6)
L2 = Fine(1, 4, 5, 24, 3)


def roll(value, by):
    return pltpu.roll(value, by % LANES, 1)


def lane_iota():
    return lax.broadcasted_iota(jnp.int32, (8, LANES), 1)


def loop(count, step, fn):
    assert count % step == 0

    def turn(i, carry):
        for k in range(step):
            fn(i * step + k)
        return carry

    lax.fori_loop(0, count // step, turn, 0)


def turns(count, most):
    return max(d for d in range(1, most + 1) if count % d == 0)


def split3(value):
    high = value.astype(BF16)
    rest = value - high.astype(F32)
    mid = rest.astype(BF16)
    low = (rest - mid.astype(F32)).astype(BF16)
    return high, mid, low


def exact_dot(value, matrix):
    total = None
    for part in split3(value):
        term = jnp.dot(part, matrix, preferred_element_type=F32)
        total = term if total is None else total + term
    return total


class Batch:
    def __init__(self):
        self.seen, self.held = {}, []

    def get(self, ref, p, x, dx, r):
        key = (id(ref), p, dx, r)
        if key not in self.seen:
            self.seen[key] = ref[p, x + dx, pl.ds(r, 8), :]
        return self.seen[key]

    def put(self, ref, p, x, dx, r, value):
        self.held.append((ref, p, x, dx, r, value))

    def flush(self):
        for ref, p, x, dx, r, value in self.held:
            ref[p, x + dx, pl.ds(r, 8), :] = value
        self.held = []


def fine_setup(lv, k_ref, w, gx, gy, size_x, size_y):
    wx, wy, wz, inv, diag = w
    h = lv.halo_inv
    lane = lane_iota()
    row = lax.broadcasted_iota(jnp.int32, (8, LANES), 0)
    parts = lv.parts
    count = lv.n + 2 * h + 1
    width = turns(count, 12 // parts)

    def planes(i):
        x = lv.off - h + width * i
        for r in lv.tiles(h):
            now = Batch()
            gy_cell = gy * lv.n + (r - ROW0) + row
            in_y = jnp.logical_and(gy_cell >= 0, gy_cell < size_y)
            cells = [[now.get(k_ref, p, x, j, r) for p in range(parts)] for j in range(width)]
            below = [roll(c[parts - 1], 1) for c in cells]
            above = [roll(c[0], -1) for c in cells]
            for j in range(width):
                gx_cell = gx * lv.n + (width * i + j - h)
                inside = jnp.logical_and(in_y, jnp.logical_and(gx_cell >= 0, gx_cell < size_x))
                first = jnp.where(lane == 0, 0.0, below[j])
                last = jnp.where(lane == LANES - 1, 0.0, above[j])
                for p in range(parts):
                    k = cells[j][p]
                    kxm, kxp = now.get(k_ref, p, x, j - 1, r), now.get(k_ref, p, x, j + 1, r)
                    kym, kyp = now.get(k_ref, p, x, j, r - 1), now.get(k_ref, p, x, j, r + 1)
                    kzm = first if p == 0 else cells[j][p - 1]
                    kzp = last if p == parts - 1 else cells[j][p + 1]
                    now.put(wx, p, x, j, r, 0.5 * (k + kxm))
                    now.put(wy, p, x, j, r, 0.5 * (k + kym))
                    down = 0.5 * (k + kzm)
                    if p == 0:
                        down = jnp.where(lane == 0, 0.0, down)
                    now.put(wz, p, x, j, r, down)
                    if p == parts - 1:
                        up = jnp.where(lane == LANES - 1, 0.0, 0.5 * (k + kzp))
                        now.put(wz, parts, x, j, r, up)
                    d = 3.0 * k + 0.5 * (((kxm + kxp) + (kym + kyp)) + (kzm + kzp))
                    now.put(diag, p, x, j, r, d)
                    now.put(inv, p, x, j, r, jnp.where(inside, 1.0 / d, 0.0))
            now.flush()

    loop(count // width, 1, planes)


def fine_sum(lv, now, v_ref, w, x, width, r):
    wx, wy, wz = w[0], w[1], w[2]
    parts = lv.parts
    cells = [[now.get(v_ref, p, x, j, r) for p in range(parts)] for j in range(width)]
    below = [roll(c[parts - 1], 1) for c in cells]
    above = [roll(c[0], -1) for c in cells]
    sums = []
    for j in range(width):
        sums.append([])
        for p in range(parts):
            along_x = now.get(wx, p, x, j, r) * now.get(v_ref, p, x, j - 1, r) + now.get(
                wx, p, x, j + 1, r
            ) * now.get(v_ref, p, x, j + 1, r)
            along_y = now.get(wy, p, x, j, r) * now.get(v_ref, p, x, j, r - 1) + now.get(
                wy, p, x, j, r + 1
            ) * now.get(v_ref, p, x, j, r + 1)
            along_z = now.get(wz, p, x, j, r) * (below[j] if p == 0 else cells[j][p - 1])
            along_z += now.get(wz, p + 1, x, j, r) * (
                above[j] if p == parts - 1 else cells[j][p + 1]
            )
            sums[j].append((along_x + along_y) + along_z)
    return sums, cells


def fine_first(lv, b_ref, w, out_ref, halo):
    inv = w[3]

    def planes(i):
        x = lv.off - halo + 2 * i
        now = Batch()
        for r in lv.tiles(halo):
            for k in range(2):
                for p in range(lv.parts):
                    value = now.get(inv, p, x, k, r) * now.get(b_ref, p, x, k, r)
                    now.put(out_ref, p, x, k, r, FIRST * value)
        now.flush()

    loop((lv.n + 2 * halo) // 2, 1, planes)


def fine_step(lv, b_ref, w, v_ref, old_ref, out_ref, halo, keep, old, step):
    inv = w[3]
    count = lv.n + 2 * halo
    width = turns(count, 8 // lv.parts)

    def planes(i):
        x = lv.off - halo + width * i
        for r in lv.tiles(halo):
            now = Batch()
            sums, cells = fine_sum(lv, now, v_ref, w, x, width, r)
            for j in range(width):
                for p in range(lv.parts):
                    value = keep * cells[j][p] + step * (
                        now.get(inv, p, x, j, r) * (now.get(b_ref, p, x, j, r) + sums[j][p])
                    )
                    if old_ref is not None:
                        value = value - old * now.get(old_ref, p, x, j, r)
                    now.put(out_ref, p, x, j, r, value)
            now.flush()

    loop(count // width, 1, planes)


def fine_restrict(lv, b_ref, w, v_ref, tmp_ref, halo=0):
    diag = w[4]
    parts = lv.parts
    count = lv.n + 2 * halo
    width = 2 * turns(count // 2, 4 // parts)

    def planes(i):
        x = lv.off - halo + width * i
        for r in lv.tiles(halo):
            now = Batch()
            sums, cells = fine_sum(lv, now, v_ref, w, x, width, r)
            for pair in range(width // 2):
                total = [None] * max(parts // 2, 1)
                for j in (2 * pair, 2 * pair + 1):
                    for p in range(parts):
                        res = (now.get(b_ref, p, x, j, r) + sums[j][p]) - now.get(
                            diag, p, x, j, r
                        ) * cells[j][p]
                        q = p // 2
                        total[q] = res if total[q] is None else total[q] + res
                for q, value in enumerate(total):
                    tmp_ref[q, width // 2 * i + pair, pl.ds(r - ROW0 + halo, 8), :] = value

    loop(count // width, 1, planes)


def fold_x(lv, k_ref, tmp_ref):
    def pair(i):
        for r in lv.tiles(0):
            for q in range(max(lv.parts // 2, 1)):
                total = None
                for p in range(lv.parts):
                    if p // 2 == q:
                        for k in range(2):
                            value = k_ref[p, lv.off + 2 * i + k, pl.ds(r, 8), :]
                            total = value if total is None else total + value
                tmp_ref[q, i, pl.ds(r - ROW0, 8), :] = total

    loop(lv.n // 2, 1, pair)


def fold_y(lv, tmp_ref, out_ref, off, scale, halo=0):
    half = lv.n // 2 + halo
    for q in range(lv.parts // 2):
        sums = []
        for i in range(half):
            even = tmp_ref[q, i, pl.ds(0, half, stride=2), :]
            odd = tmp_ref[q, i, pl.ds(1, half, stride=2), :]
            sums.append(scale * (even + odd))
        for i in range(half):
            out_ref[q, off - halo // 2 + i, pl.ds(ROW0 - halo // 2, half), :] = sums[i]


def fold_z(tmp_ref, left_ref, matrix, scale):
    for i in range(2):
        for j in range(2):
            row = tmp_ref[0, i, pl.ds(2 * j, 1), :] + tmp_ref[0, i, pl.ds(2 * j + 1, 1), :]
            left_ref[pl.ds(i, 1), pl.ds(LANES * j, LANES)] = scale * row
    return exact_dot(left_ref[...], matrix)


def fine_correct(lv, next_lv, e_ref, s_ref, t_ref, halo):
    next_halo = -(-halo // 2)
    row_lo = ROW0 - next_halo
    rows = next_lv.n + 2 * next_halo
    starts = [row_lo + 8 * t for t in range(-(-rows // 8))]
    if len(starts) == 2:
        starts = [4, 12]

    def plane(i):
        big = next_lv.off - next_halo + i
        for q in range(next_lv.parts):
            for r in starts:
                e = e_ref[q, big, pl.ds(r, 8), :]
                base = 2 * (r - ROW0) + ROW0
                held = []
                for p in (2 * q, 2 * q + 1):
                    for k in range(2):
                        x = lv.off + 2 * (i - next_halo) + k
                        for c in range(2):
                            at = (p, x, pl.ds(base + c, 8, stride=2), slice(None))
                            held.append((at, s_ref[at] + e))
                for at, value in held:
                    t_ref[at] = value

    loop(next_lv.n + 2 * next_halo, 1, plane)


def coarse_rolls(lv, ref, first, count, r):
    return [roll(ref[first - 1 + i, pl.ds(r, 8), :], LANES // 2) for i in range(count + 2)]


def coarse_beside(lv, ref, first, count, r):
    out = []
    low = lane_iota() < LANES // 2
    turned = coarse_rolls(lv, ref, first, count, r) if lv.split else None
    for i in range(count):
        y = first + i
        v = ref[y, pl.ds(r, 8), :]
        xm, xp = ref[y, pl.ds(r - 1, 8), :], ref[y, pl.ds(r + 1, 8), :]
        if lv.split:
            ym = jnp.where(low, turned[i], turned[i + 1])
            yp = jnp.where(low, turned[i + 1], turned[i + 2])
        else:
            ym, yp = ref[y - 1, pl.ds(r, 8), :], ref[y + 1, pl.ds(r, 8), :]
        out.append((v, xm, xp, ym, yp, roll(v, lv.step), roll(v, -lv.step)))
    return out


def coarse_setup(lv, k_ref, w):
    lane = lane_iota() % (LANES // 2)
    bottom, top = lane < lv.step, lane >= LANES // 2 - lv.step
    group = 4 if lv.split else 8

    def planes(i):
        first = 1 + group * i
        for r in lv.tiles:
            for j, (k, xm, xp, ym, yp, zm, zp) in enumerate(
                coarse_beside(lv, k_ref, first, group, r)
            ):
                y = first + j
                zm, zp = jnp.where(bottom, 0.0, zm), jnp.where(top, 0.0, zp)
                w[0][0, y, pl.ds(r, 8), :] = 0.5 * (k + xm)
                w[0][1, y, pl.ds(r, 8), :] = 0.5 * (k + xp)
                w[0][2, y, pl.ds(r, 8), :] = 0.5 * (k + ym)
                w[0][3, y, pl.ds(r, 8), :] = 0.5 * (k + yp)
                w[0][4, y, pl.ds(r, 8), :] = jnp.where(bottom, 0.0, 0.5 * (k + zm))
                w[0][5, y, pl.ds(r, 8), :] = jnp.where(top, 0.0, 0.5 * (k + zp))
                d = 3.0 * k + 0.5 * (((xm + xp) + (ym + yp)) + (zm + zp))
                w[0][6, y, pl.ds(r, 8), :] = d
                w[0][7, y, pl.ds(r, 8), :] = 1.0 / d

    loop(lv.planes // group, 1, planes)


def coarse_apply(lv, w, v_ref, out_ref, fn):
    group = 4 if lv.split else 8

    def planes(i):
        first = 1 + group * i
        held = []
        for r in lv.tiles:
            for j, beside in enumerate(coarse_beside(lv, v_ref, first, group, r)):
                y = first + j
                terms = [w[0][f, y, pl.ds(r, 8), :] * beside[1 + f] for f in range(6)]
                total = ((terms[0] + terms[1]) + (terms[2] + terms[3])) + (terms[4] + terms[5])
                held.append((y, r, fn(y, r, beside[0], total)))
        for y, r, value in held:
            out_ref[y, pl.ds(r, 8), :] = value

    loop(lv.planes // group, 1, planes)


def coarse_first(lv, b_ref, w, out_ref):
    def plane(i):
        for r in lv.tiles:
            at = (1 + i, pl.ds(r, 8), slice(None))
            out_ref[at] = FIRST * (w[0][7, 1 + i, pl.ds(r, 8), :] * b_ref[at])

    loop(lv.planes, 4, plane)


def coarse_step(lv, b_ref, w, v_ref, old_ref, out_ref, keep, old, step):
    def tile(y, r, v, total):
        at = (y, pl.ds(r, 8), slice(None))
        value = keep * v + step * (w[0][7, y, pl.ds(r, 8), :] * (b_ref[at] + total))
        if old_ref is not None:
            value = value - old * old_ref[at]
        return value

    coarse_apply(lv, w, v_ref, out_ref, tile)


def coarse_residual(lv, b_ref, w, v_ref, out_ref):
    def tile(y, r, v, total):
        at = (y, pl.ds(r, 8), slice(None))
        return (b_ref[at] + total) - w[0][6, y, pl.ds(r, 8), :] * v

    coarse_apply(lv, w, v_ref, out_ref, tile)


def coarse_fold(lv, next_lv, ref, out_ref, scale):
    lane = lane_iota()
    even = (lane // lv.step) % 2 == 0
    joined = lv.planes // next_lv.planes

    group = 8

    def planes(i):
        totals = []
        for k in range(group):
            for r in next_lv.tiles:
                base = ROW0 + 2 * (r - ROW0)
                y = 1 + joined * (group * i + k)
                terms = [
                    ref[y + j, pl.ds(base + c, 8, stride=2), :]
                    for j in range(joined)
                    for c in range(2)
                ]
                total = terms[0] + terms[1]
                if joined == 2:
                    total = total + (terms[2] + terms[3])
                totals.append(total)
        if lv.split:
            totals = [total + roll(total, LANES // 2) for total in totals]
        totals = [
            scale * (total + jnp.where(even, roll(total, -lv.step), roll(total, lv.step)))
            for total in totals
        ]
        for k in range(group):
            for j, r in enumerate(next_lv.tiles):
                out_ref[1 + group * i + k, pl.ds(r, 8), :] = totals[k * len(next_lv.tiles) + j]

    loop(next_lv.planes // group, 1, planes)


def coarse_correct(lv, next_lv, e_ref, s_ref, t_ref):
    joined = lv.planes // next_lv.planes

    def plane(i):
        for r in next_lv.tiles:
            e = e_ref[1 + i, pl.ds(r, 8), :]
            base = ROW0 + 2 * (r - ROW0)
            held = []
            for j in range(joined):
                for c in range(2):
                    at = (1 + joined * i + j, pl.ds(base + c, 8, stride=2), slice(None))
                    held.append((at, s_ref[at] + e))
            for at, value in held:
                t_ref[at] = value

    loop(next_lv.planes, 4, plane)


def zero_margin(lv, ref):
    zero = jnp.zeros((8, LANES), F32)
    for y in (0, lv.planes + 1):
        for r in lv.tiles:
            ref[y, pl.ds(r, 8), :] = zero

    def plane(y):
        ref[y, pl.ds(0, 8), :] = zero
        ref[y, pl.ds(ROW0 + lv.n, 8), :] = zero

    loop(lv.planes + 2, 1, plane)


class Links:
    def __init__(self, send, recv):
        self.send, self.recv, self.used = send, recv, 0

    def group(self):
        index = self.used
        self.used += 1

        def copy(src, dst, device):
            return pltpu.make_async_remote_copy(
                src_ref=src,
                dst_ref=dst,
                send_sem=self.send.at[index],
                recv_sem=self.recv.at[index],
                device_id=device,
                device_id_type=MESH,
            )

        return copy


class Halo:
    def __init__(self, place, links, groups):
        gx, gy, nx, ny = place
        self.copies, self.waits = [], []
        for copies, whole in groups:
            copy = links.group()
            for (dx, dy), src, dst in copies:
                device = (lax.rem(gx + dx + nx, nx), lax.rem(gy + dy + ny, ny))
                self.copies.append(copy(src, dst, device))
            self.waits.append(copy(whole, whole, device))

    def start(self):
        for copy in self.copies:
            copy.start()

    def wait_recv(self):
        for wait in self.waits:
            wait.wait_recv()

    def wait_send(self):
        for wait in self.waits:
            wait.wait_send()


def there(place, dx, dy):
    gx, gy, nx, ny = place
    ok = None
    for at, by, size in ((gx, dx, nx), (gy, dy, ny)):
        if by:
            test = at + by < size if by > 0 else at + by >= 0
            ok = test if ok is None else jnp.logical_and(ok, test)
    return True if ok is None else ok


class Rim:
    def __init__(self, lv, halo, refs):
        self.lv, self.halo = lv, halo
        self.send_x, self.send_y, self.recv_x, self.recv_y = refs

    @staticmethod
    def scratch(lv, halo):
        n, parts = lv.n, lv.parts
        return [
            pltpu.VMEM((2, parts, halo, n, LANES), F32),
            pltpu.VMEM((2, parts, n, halo, LANES), F32),
            pltpu.VMEM((2, parts, halo, n, LANES), F32),
            pltpu.VMEM((2, parts, n + 2 * halo, halo, LANES), F32),
        ]

    def pack(self, ref):
        lv, h = self.lv, self.halo
        for side, start in ((0, lv.off), (1, lv.off + lv.n - h)):
            for p in range(lv.parts):
                for i in range(h):
                    self.send_x[side, p, i] = ref[p, start + i, pl.ds(ROW0, lv.n), :]

        def plane(i):
            for p in range(lv.parts):
                self.send_y[0, p, i] = ref[p, lv.off + i, pl.ds(ROW0, h), :]
                self.send_y[1, p, i] = ref[p, lv.off + i, pl.ds(ROW0 + lv.n - h, h), :]

        loop(lv.n, 2, plane)

    def exchange(self, place, links):
        h, n = self.halo, self.lv.n
        faces, others = [], []
        for dx, dy in NEIGHBOURS:
            if dy == 0:
                src = self.send_x.at[1 if dx > 0 else 0]
                faces.append(((dx, dy), src, self.recv_x.at[0 if dx > 0 else 1]))
                continue
            src = self.send_y.at[1 if dy > 0 else 0]
            dst = self.recv_y.at[0 if dy > 0 else 1]
            if dx == 0:
                dst = dst.at[:, h : h + n]
            elif dx > 0:
                src, dst = src.at[:, n - h : n], dst.at[:, 0:h]
            else:
                src, dst = src.at[:, 0:h], dst.at[:, h + n : n + 2 * h]
            others.append(((dx, dy), src, dst))
        return Halo(place, links, [(others, self.recv_y), (faces, self.recv_x)])

    def unpack(self, ref, place):
        lv, h, n = self.lv, self.halo, self.lv.n
        for side, start, dx in ((0, lv.off - h, -1), (1, lv.off + n, 1)):
            ok = there(place, dx, 0)
            for p in range(lv.parts):
                for i in range(h):
                    value = self.recv_x[side, p, i]
                    ref[p, start + i, pl.ds(ROW0, n), :] = jnp.where(ok, value, 0.0)

        gx, gy, nx, ny = place

        def plane(i):
            cell = gx * n + (i - h)
            in_x = jnp.logical_and(cell >= 0, cell < nx * n)
            for side, row, dy in ((0, ROW0 - h, -1), (1, ROW0 + n, 1)):
                ok = jnp.logical_and(in_x, there(place, 0, dy))
                for p in range(lv.parts):
                    value = self.recv_y[side, p, i]
                    ref[p, lv.off - h + i, pl.ds(row, h), :] = jnp.where(ok, value, 0.0)

        loop(n + 2 * h, 2, plane)


class Blocks:
    def __init__(self, lv, refs):
        self.lv = lv
        self.send, self.recv = refs

    @staticmethod
    def scratch(lv):
        n = lv.n
        return [pltpu.VMEM((n, n, LANES), F32), pltpu.VMEM((8, n, n, LANES), F32)]

    def pack(self, ref):
        lv = self.lv
        for i in range(lv.n):
            self.send[i] = ref[0, lv.off + i, pl.ds(ROW0, lv.n), :]

    def exchange(self, place, links):
        n = self.lv.n
        copies = []
        for dx, dy in NEIGHBOURS:
            slot = (1 + dy) * 3 + 1 + dx
            slot -= 1 if slot > 4 else 0
            copies.append(((dx, dy), self.send, self.recv.at[slot]))
        return Halo(place, links, [(copies, self.recv)])

    def unpack(self, ref, place):
        lv, n = self.lv, self.lv.n
        for dx, dy in NEIGHBOURS:
            slot = (1 + dy) * 3 + 1 + dx
            slot -= 1 if slot > 4 else 0
            ok = there(place, -dx, -dy)
            for k in range(n):
                ref[0, lv.off - n * dx + k, pl.ds(ROW0 - n * dy, n), :] = jnp.where(
                    ok, self.recv[slot, k], 0.0
                )


class Gather:
    def __init__(self, place, links, piece_ref, whole_ref):
        gx, gy, nx, ny = place
        self.place = place
        self.piece, self.whole = piece_ref, whole_ref
        mine = piece_ref.at[gx]
        copy = links.group()
        self.along_x = [copy(mine, mine, (lax.rem(gx + d, nx), gy)) for d in range(1, nx)]
        rest = piece_ref.at[0 : nx - 1]
        self.wait_x = copy(rest, rest, (lax.rem(gx + 1, nx), gy))
        slab = whole_ref.at[1 + gy, pl.ds(ROW0, 2 * nx), :]
        copy = links.group()
        self.along_y = [copy(slab, slab, (gx, lax.rem(gy + d, ny))) for d in range(1, ny)]
        rest = whole_ref.at[1:ny, pl.ds(ROW0, 2 * nx), :]
        self.wait_y = copy(rest, rest, (gx, lax.rem(gy + 1, ny)))

    def start_x(self, value):
        gx = self.place[0]
        self.piece[gx] = value
        for copy in self.along_x:
            copy.start()

    def start_y(self):
        gx, gy, nx, ny = self.place
        self.wait_x.wait_recv()
        for i in range(nx):
            self.whole[1 + gy, pl.ds(ROW0 + 2 * i, 2), :] = self.piece[i]
        for copy in self.along_y:
            copy.start()

    def finish(self):
        self.wait_y.wait_recv()

    def wait_send(self):
        self.wait_x.wait_send()
        self.wait_y.wait_send()


def scratch_shapes(nx, ny):
    l3, l4, l5 = coarse_levels(nx, ny)
    shapes = {}
    for name in ("raw_k", "raw_b", "out"):
        shapes[name] = pltpu.VMEM((L0.n, L0.n, L0.parts * LANES), F32)
    shapes["perm"] = pltpu.VMEM((512, 512), BF16)
    shapes["back"] = pltpu.VMEM((512, 512), BF16)
    shapes["left"] = pltpu.VMEM((8, 2 * LANES), F32)
    for i, lv in enumerate((L0, L1, L2)):
        for name in ("k", "b", "wx", "wy", "inv", "diag", "x", "s", "t"):
            shapes[name + str(i)] = pltpu.VMEM(lv.shape, F32)
        shapes["wz" + str(i)] = pltpu.VMEM((lv.parts + 1,) + lv.shape[1:], F32)
        shapes["tmp" + str(i)] = pltpu.VMEM((max(lv.parts // 2, 1), 8, 16, LANES), F32)
    shapes["e2"] = pltpu.VMEM((6, L2.rows, LANES), F32)
    for i, lv in ((3, l3), (4, l4), (5, l5)):
        for name in ("k", "b", "x", "s", "t"):
            shapes[name + str(i)] = pltpu.VMEM(lv.shape, F32)
        shapes["w" + str(i)] = pltpu.VMEM((8,) + lv.shape, F32)
    for name, lv, halo in (("rk0", L0, 3), ("rb0", L0, 2), ("rs0", L0, 2), ("rk1", L1, 7), ("rb1", L1, 6)):
        for j, shape in enumerate(Rim.scratch(lv, halo)):
            shapes[name + "_" + str(j)] = shape
    for name in ("rk2", "rb2", "rs2"):
        for j, shape in enumerate(Blocks.scratch(L2)):
            shapes[name + "_" + str(j)] = shape
    for name in ("pk3", "pb3"):
        shapes[name] = pltpu.VMEM((nx, 2, LANES), F32)
    copies = 5 * 2 + 3 + 2 * 2
    shapes["send"] = pltpu.SemaphoreType.DMA((copies,))
    shapes["recv"] = pltpu.SemaphoreType.DMA((copies,))
    shapes["local"] = pltpu.SemaphoreType.DMA((4,))
    return shapes


def coarse_levels(nx, ny):
    return (
        Coarse(ny, 2 * nx, 1, True),
        Coarse(ny, nx, 2, False),
        Coarse(ny // 2, nx // 2, 4, False),
    )


def kernel(nx, ny, names, b_in, k_in, out_ref, *refs):
    m = dict(zip(names, refs))
    gx, gy = lax.axis_index("gx"), lax.axis_index("gy")
    place = (gx, gy, nx, ny)
    l3, l4, l5 = coarse_levels(nx, ny)
    links = Links(m["send"], m["recv"])

    def pair(name, cls, *args):
        refs = [m[key] for key in names if key.startswith(name + "_")]
        return cls(*args, refs)

    rk0, rb0, rs0 = (pair(name, Rim, L0, h) for name, h in (("rk0", 3), ("rb0", 2), ("rs0", 2)))
    rk1, rb1 = (pair(name, Rim, L1, h) for name, h in (("rk1", 7), ("rb1", 6)))
    rk2, rb2, rs2 = (pair(name, Blocks, L2) for name in ("rk2", "rb2", "rs2"))
    hk0, hb0, hs0, hk1, hb1, hk2, hb2, hs2 = (
        rim.exchange(place, links) for rim in (rk0, rb0, rs0, rk1, rb1, rk2, rb2, rs2)
    )
    gk3 = Gather(place, links, m["pk3"], m["k3"])
    gb3 = Gather(place, links, m["pb3"], m["b3"])

    load_k = pltpu.make_async_copy(k_in, m["raw_k"], m["local"].at[0])
    load_b = pltpu.make_async_copy(b_in, m["raw_b"], m["local"].at[1])
    load_k.start()
    load_b.start()

    barrier = pltpu.get_barrier_semaphore()
    peers = [(dx, dy) for dx, dy in NEIGHBOURS]
    peers += [(d, 0) for d in range(2, nx - 1)] + [(0, d) for d in range(2, ny - 1)]
    for dx, dy in peers:
        pl.semaphore_signal(
            barrier,
            inc=1,
            device_id=(lax.rem(gx + dx + nx, nx), lax.rem(gy + dy + ny, ny)),
            device_id_type=MESH,
        )

    def one(rows, cols, test):
        at = lax.broadcasted_iota(jnp.int32, (rows, cols), 0)
        to = lax.broadcasted_iota(jnp.int32, (rows, cols), 1)
        return jnp.where(test(at, to), 1.0, 0.0).astype(BF16)

    def fill(i):
        start = pl.multiple_of(i * 64, 64)
        m["perm"][pl.ds(start, 64), :] = one(
            64, 512, lambda at, to: at + start == 4 * (to % LANES) + to // LANES
        )

    def fill_back(i):
        start = pl.multiple_of(i * 64, 64)
        m["back"][pl.ds(start, 64), :] = one(
            64, 512, lambda at, to: to == 4 * ((at + start) % LANES) + (at + start) // LANES
        )

    loop(8, 1, fill)
    m["left"][...] = jnp.zeros_like(m["left"])
    fold = one(
        2 * LANES,
        LANES,
        lambda at, to: jnp.logical_and(at // LANES == to // 64, (at % LANES) // 2 == to % 64),
    )
    unfold = one(
        LANES,
        2 * LANES,
        lambda at, to: jnp.logical_and(to // LANES == at // 64, (to % LANES) // 2 == at % 64),
    )

    def reorder(raw, ref):
        half = L0.n // 2
        for c in range(2):
            value = raw[c * half : (c + 1) * half].reshape(half * L0.n, 512)
            moved = exact_dot(value, m["perm"][...])
            for p in range(L0.parts):
                ref[p, pl.ds(L0.off + c * half, half), pl.ds(ROW0, L0.n), :] = moved[
                    :, p * LANES : (p + 1) * LANES
                ].reshape(half, L0.n, LANES)

    load_k.wait()
    reorder(m["raw_k"], m["k0"])
    rk0.pack(m["k0"])
    pl.semaphore_wait(barrier, len(peers))
    hk0.start()
    load_b.wait()
    reorder(m["raw_b"], m["b0"])
    rb0.pack(m["b0"])
    hb0.start()

    fold_x(L0, m["k0"], m["tmp0"])
    fold_y(L0, m["tmp0"], m["k1"], L1.off, 0.125)
    rk1.pack(m["k1"])
    hk1.start()
    fold_x(L1, m["k1"], m["tmp1"])
    fold_y(L1, m["tmp1"], m["k2"], L2.off, 0.125)
    rk2.pack(m["k2"])
    hk2.start()
    fold_x(L2, m["k2"], m["tmp2"])
    gk3.start_x(fold_z(m["tmp2"], m["left"], fold, 0.125)[0:2])
    for lv, i in ((l3, 3), (l4, 4), (l5, 5)):
        for name in ("k", "x", "s", "t"):
            zero_margin(lv, m[name + str(i)])
    loop(8, 1, fill_back)

    weights = [
        tuple(m[name + str(i)] for name in ("wx", "wy", "wz", "inv", "diag")) for i in range(3)
    ]
    sizes = [(nx * lv.n, ny * lv.n) for lv in (L0, L1, L2)]
    w3, w4, w5 = (m["w3"],), (m["w4"],), (m["w5"],)

    hk0.wait_recv()
    rk0.unpack(m["k0"], place)
    fine_setup(L0, m["k0"], weights[0], gx, gy, *sizes[0])
    hb0.wait_recv()
    rb0.unpack(m["b0"], place)
    fine_first(L0, m["b0"], weights[0], m["x0"], 2)
    fine_step(L0, m["b0"], weights[0], m["x0"], None, m["s0"], 1, KEEP, OLD, STEP)
    fine_restrict(L0, m["b0"], weights[0], m["s0"], m["tmp0"])
    fold_y(L0, m["tmp0"], m["b1"], L1.off, 0.5)
    rb1.pack(m["b1"])
    hb1.start()
    rs0.pack(m["s0"])
    hs0.start()

    gk3.start_y()
    hk1.wait_recv()
    rk1.unpack(m["k1"], place)
    fine_setup(L1, m["k1"], weights[1], gx, gy, *sizes[1])
    hk2.wait_recv()
    rk2.unpack(m["k2"], place)
    fine_setup(L2, m["k2"], weights[2], gx, gy, *sizes[2])

    hb1.wait_recv()
    rb1.unpack(m["b1"], place)
    fine_first(L1, m["b1"], weights[1], m["x1"], 6)
    fine_step(L1, m["b1"], weights[1], m["x1"], None, m["s1"], 5, KEEP, OLD, STEP)
    fine_restrict(L1, m["b1"], weights[1], m["s1"], m["tmp1"], 4)
    fold_y(L1, m["tmp1"], m["b2"], L2.off, 0.5, 4)

    fine_first(L2, m["b2"], weights[2], m["x2"], 2)
    fine_step(L2, m["b2"], weights[2], m["x2"], None, m["s2"], 1, KEEP, OLD, STEP)
    fine_restrict(L2, m["b2"], weights[2], m["s2"], m["tmp2"])
    gb3.start_x(fold_z(m["tmp2"], m["left"], fold, 0.5)[0:2])
    rb2.pack(m["b2"])
    hb2.start()
    rs2.pack(m["s2"])
    hs2.start()

    gk3.finish()
    coarse_setup(l3, m["k3"], w3)
    gb3.start_y()
    coarse_fold(l3, l4, m["k3"], m["k4"], 0.125)
    coarse_setup(l4, m["k4"], w4)
    coarse_fold(l4, l5, m["k4"], m["k5"], 0.125)
    coarse_setup(l5, m["k5"], w5)
    for part in (hs0, hb2, hs2):
        part.wait_recv()
        part.wait_send()
    rs0.unpack(m["s0"], place)
    rb2.unpack(m["b2"], place)
    rs2.unpack(m["s2"], place)
    gb3.finish()

    coarse_first(l3, m["b3"], w3, m["x3"])
    coarse_step(l3, m["b3"], w3, m["x3"], None, m["s3"], KEEP, OLD, STEP)
    coarse_residual(l3, m["b3"], w3, m["s3"], m["t3"])
    coarse_fold(l3, l4, m["t3"], m["b4"], 0.5)
    coarse_first(l4, m["b4"], w4, m["x4"])
    coarse_step(l4, m["b4"], w4, m["x4"], None, m["s4"], KEEP, OLD, STEP)
    coarse_residual(l4, m["b4"], w4, m["s4"], m["t4"])
    coarse_fold(l4, l5, m["t4"], m["b5"], 0.5)
    coarse_first(l5, m["b5"], w5, m["x5"])
    now, old, spare = m["x5"], None, [m["s5"], m["t5"]]
    rho = RHO0
    for _ in range(COARSE_ITERS - 1):
        rho_new = 1.0 / (2.0 * SIGMA - rho)
        keep = 1.0 + rho_new * rho - 2.0 * rho_new / RADIUS
        out = spare.pop(0)
        coarse_step(l5, m["b5"], w5, now, old, out, keep, rho_new * rho, 2.0 * rho_new / RADIUS)
        if old is not None:
            spare.append(old)
        now, old, rho = out, now, rho_new
    coarse_correct(l4, l5, now, m["s4"], m["t4"])
    coarse_step(l4, m["b4"], w4, m["t4"], None, m["x4"], 1.0 - FIRST, 0.0, FIRST)
    coarse_step(l4, m["b4"], w4, m["x4"], m["t4"], m["s4"], KEEP, OLD, STEP)
    coarse_correct(l3, l4, m["s4"], m["s3"], m["t3"])
    coarse_step(l3, m["b3"], w3, m["t3"], None, m["x3"], 1.0 - FIRST, 0.0, FIRST)
    coarse_step(l3, m["b3"], w3, m["x3"], m["t3"], m["s3"], KEEP, OLD, STEP)

    near = jnp.concatenate(
        [m["s3"][gy + d, pl.ds(2 * gx + ROW0 - 2, 8), :] for d in range(3)], axis=0
    )
    wide = exact_dot(near, unfold)
    for d in range(3):
        for i in range(6):
            for a in range(2):
                row = wide[8 * d + i : 8 * d + i + 1, a * LANES : (a + 1) * LANES]
                m["e2"][i, pl.ds(ROW0 - 4 + 4 * d + 2 * a, 2), :] = jnp.broadcast_to(
                    row, (2, LANES)
                )
    for i in range(6):
        for k in range(2):
            x = L2.off - 4 + 2 * i + k
            for r in L2.tiles(4):
                m["t2"][0, x, pl.ds(r, 8), :] = (
                    m["s2"][0, x, pl.ds(r, 8), :] + m["e2"][i, pl.ds(r, 8), :]
                )
    fine_step(L2, m["b2"], weights[2], m["t2"], None, m["x2"], 3, 1.0 - FIRST, 0.0, FIRST)
    fine_step(L2, m["b2"], weights[2], m["x2"], m["t2"], m["s2"], 2, KEEP, OLD, STEP)

    fine_correct(L1, L2, m["s2"], m["s1"], m["t1"], 3)
    fine_step(L1, m["b1"], weights[1], m["t1"], None, m["x1"], 2, 1.0 - FIRST, 0.0, FIRST)
    fine_step(L1, m["b1"], weights[1], m["x1"], m["t1"], m["s1"], 1, KEEP, OLD, STEP)

    fine_correct(L0, L1, m["s1"], m["s0"], m["t0"], 2)
    fine_step(L0, m["b0"], weights[0], m["t0"], None, m["x0"], 1, 1.0 - FIRST, 0.0, FIRST)
    fine_step(L0, m["b0"], weights[0], m["x0"], m["t0"], m["s0"], 0, KEEP, OLD, STEP)

    half = L0.n // 2
    stores = []
    for c in range(2):
        value = jnp.concatenate(
            [
                m["s0"][p, pl.ds(L0.off + c * half, half), pl.ds(ROW0, L0.n), :].reshape(
                    half * L0.n, LANES
                )
                for p in range(L0.parts)
            ],
            axis=1,
        )
        moved = exact_dot(value, m["back"][...])
        m["out"][c * half : (c + 1) * half] = moved.reshape(half, L0.n, 512)
        stores.append(
            pltpu.make_async_copy(
                m["out"].at[c * half : (c + 1) * half],
                out_ref.at[c * half : (c + 1) * half],
                m["local"].at[2 + c],
            )
        )
        stores[c].start()
    for part in (hk0, hb0, hk1, hb1, hk2, gk3, gb3):
        part.wait_send()
    for store in stores:
        store.wait()


def solution(mesh):
    nx, ny = mesh.shape["gx"], mesh.shape["gy"]
    shapes = scratch_shapes(nx, ny)

    def body(right_side, coefficient):
        return pl.pallas_call(
            functools.partial(kernel, nx, ny, list(shapes)),
            out_shape=jax.ShapeDtypeStruct(right_side.shape, F32),
            in_specs=[pl.BlockSpec(memory_space=pl.ANY)] * 2,
            out_specs=pl.BlockSpec(memory_space=pl.ANY),
            scratch_shapes=list(shapes.values()),
            compiler_params=pltpu.CompilerParams(
                collective_id=0, has_side_effects=True, vmem_limit_bytes=56 * 1024 * 1024
            ),
        )(right_side, coefficient)

    return jax.shard_map(
        body,
        mesh=mesh,
        in_specs=(P("gx", "gy", None), P("gx", "gy", None)),
        out_specs=P("gx", "gy", None),
        check_vma=False,
    )
```

```python
import functools

import jax
import jax.numpy as jnp
from jax import lax
from jax.experimental import pallas as pl
from jax.experimental.pallas import tpu as pltpu
from jax.sharding import PartitionSpec as P

MESH = pl.DeviceIdType.MESH
F32 = jnp.float32
BF16 = jnp.bfloat16

CENTRE = 1.15
RADIUS = 0.85
COARSE_ITERS = 6
SIGMA = CENTRE / RADIUS
RHO0 = 1.0 / SIGMA
RHO1 = 1.0 / (2.0 * SIGMA - RHO0)
KEEP = 1.0 + RHO1 * RHO0 - 2.0 * RHO1 / RADIUS
OLD = RHO1 * RHO0
STEP = 2.0 * RHO1 / RADIUS
FIRST = 1.0 / CENTRE

NEIGHBOURS = [(dx, dy) for dx in (-1, 0, 1) for dy in (-1, 0, 1) if (dx, dy) != (0, 0)]
ROW0 = 8
LANES = 128


class Fine:
    def __init__(self, parts, n, off, rows, halo_inv):
        self.parts, self.n, self.off, self.rows, self.halo_inv = parts, n, off, rows, halo_inv
        self.planes = n + 2 * off
        self.shape = (parts, self.planes, rows, LANES)

    def tiles(self, halo):
        low, count = ROW0 - halo, self.n + 2 * halo
        if halo == 0:
            return [low + 8 * t for t in range(-(-count // 8))]
        if count % 8 == 0:
            return [low + 8 * t for t in range(count // 8)]
        tiles = -(-count // 8)
        low = max(1, low - (tiles * 8 - count) // 2)
        return [low + 8 * t for t in range(tiles)]


class Coarse:
    def __init__(self, planes, n, step, split):
        self.planes, self.n, self.step, self.split = planes, n, step, split
        self.shape = (planes + 2, n + 16, LANES)
        self.tiles = [ROW0 + 8 * t for t in range(n // 8)]


L0 = Fine(4, 16, 4, 32, 2)
L1 = Fine(2, 8, 8, 32, 6)
L2 = Fine(1, 4, 5, 24, 3)


def roll(value, by):
    return pltpu.roll(value, by % LANES, 1)


def lane_iota():
    return lax.broadcasted_iota(jnp.int32, (8, LANES), 1)


def loop(count, step, fn):
    assert count % step == 0

    def turn(i, carry):
        for k in range(step):
            fn(i * step + k)
        return carry

    lax.fori_loop(0, count // step, turn, 0)


def turns(count, most):
    return max(d for d in range(1, most + 1) if count % d == 0)


def split3(value):
    high = value.astype(BF16)
    rest = value - high.astype(F32)
    mid = rest.astype(BF16)
    low = (rest - mid.astype(F32)).astype(BF16)
    return high, mid, low


def exact_dot(value, matrix):
    rows = value.shape[0]
    moved = jnp.dot(
        jnp.concatenate(split3(value), axis=0), matrix, preferred_element_type=F32
    )
    return (moved[:rows] + moved[rows : 2 * rows]) + moved[2 * rows :]


def one(rows, cols, test):
    at = lax.broadcasted_iota(jnp.int32, (rows, cols), 0)
    to = lax.broadcasted_iota(jnp.int32, (rows, cols), 1)
    return jnp.where(test(at, to), 1.0, 0.0).astype(BF16)


class Batch:
    def __init__(self):
        self.seen, self.held = {}, []

    def get(self, ref, p, x, dx, r):
        key = (id(ref), p, dx, r)
        if key not in self.seen:
            self.seen[key] = ref[p, x + dx, pl.ds(r, 8), :]
        return self.seen[key]

    def put(self, ref, p, x, dx, r, value):
        self.held.append((ref, p, x, dx, r, value))

    def flush(self):
        for ref, p, x, dx, r, value in self.held:
            ref[p, x + dx, pl.ds(r, 8), :] = value
        self.held = []


def fine_setup(lv, k_ref, w, gx, gy, size_x, size_y):
    wx, wy, wz, inv, diag = w
    h = lv.halo_inv
    lane = lane_iota()
    row = lax.broadcasted_iota(jnp.int32, (8, LANES), 0)
    parts = lv.parts
    start, count, tiles = -h, lv.n + 2 * h + 1, lv.tiles(h)
    width = turns(count, 12 // parts)

    def planes(i):
        x = lv.off + start + width * i
        for r in tiles:
            now = Batch()
            gy_cell = gy * lv.n + (r - ROW0) + row
            in_y = jnp.logical_and(gy_cell >= 0, gy_cell < size_y)
            cells = [[now.get(k_ref, p, x, j, r) for p in range(parts)] for j in range(width)]
            below = [roll(c[parts - 1], 1) for c in cells]
            above = [roll(c[0], -1) for c in cells]
            for j in range(width):
                gx_cell = gx * lv.n + (width * i + j + start)
                inside = jnp.logical_and(in_y, jnp.logical_and(gx_cell >= 0, gx_cell < size_x))
                first = jnp.where(lane == 0, 0.0, below[j])
                last = jnp.where(lane == LANES - 1, 0.0, above[j])
                for p in range(parts):
                    k = cells[j][p]
                    kxm, kxp = now.get(k_ref, p, x, j - 1, r), now.get(k_ref, p, x, j + 1, r)
                    kym, kyp = now.get(k_ref, p, x, j, r - 1), now.get(k_ref, p, x, j, r + 1)
                    kzm = first if p == 0 else cells[j][p - 1]
                    kzp = last if p == parts - 1 else cells[j][p + 1]
                    now.put(wx, p, x, j, r, 0.5 * (k + kxm))
                    now.put(wy, p, x, j, r, 0.5 * (k + kym))
                    down = 0.5 * (k + kzm)
                    if p == 0:
                        down = jnp.where(lane == 0, 0.0, down)
                    now.put(wz, p, x, j, r, down)
                    if p == parts - 1:
                        up = jnp.where(lane == LANES - 1, 0.0, 0.5 * (k + kzp))
                        now.put(wz, parts, x, j, r, up)
                    d = 3.0 * k + 0.5 * (((kxm + kxp) + (kym + kyp)) + (kzm + kzp))
                    now.put(diag, p, x, j, r, d)
                    now.put(inv, p, x, j, r, jnp.where(inside, 1.0 / d, 0.0))
            now.flush()

    loop(count // width, 1, planes)


def fine_sum(lv, now, v_ref, w, x, width, r):
    wx, wy, wz = w[0], w[1], w[2]
    parts = lv.parts
    cells = [[now.get(v_ref, p, x, j, r) for p in range(parts)] for j in range(width)]
    below = [roll(c[parts - 1], 1) for c in cells]
    above = [roll(c[0], -1) for c in cells]
    sums = []
    for j in range(width):
        sums.append([])
        for p in range(parts):
            along_x = now.get(wx, p, x, j, r) * now.get(v_ref, p, x, j - 1, r) + now.get(
                wx, p, x, j + 1, r
            ) * now.get(v_ref, p, x, j + 1, r)
            along_y = now.get(wy, p, x, j, r) * now.get(v_ref, p, x, j, r - 1) + now.get(
                wy, p, x, j, r + 1
            ) * now.get(v_ref, p, x, j, r + 1)
            along_z = now.get(wz, p, x, j, r) * (below[j] if p == 0 else cells[j][p - 1])
            along_z += now.get(wz, p + 1, x, j, r) * (
                above[j] if p == parts - 1 else cells[j][p + 1]
            )
            sums[j].append((along_x + along_y) + along_z)
    return sums, cells


def fine_first(lv, b_ref, w, out_ref, halo):
    inv = w[3]

    def planes(i):
        x = lv.off - halo + 2 * i
        now = Batch()
        for r in lv.tiles(halo):
            for k in range(2):
                for p in range(lv.parts):
                    value = now.get(inv, p, x, k, r) * now.get(b_ref, p, x, k, r)
                    now.put(out_ref, p, x, k, r, FIRST * value)
        now.flush()

    loop((lv.n + 2 * halo) // 2, 1, planes)


def fine_step(
    lv, b_ref, w, v_ref, old_ref, out_ref, halo, keep, old, step, start=None, count=None
):
    inv = w[3]
    if count is None:
        start, count = -halo, lv.n + 2 * halo
    width = turns(count, 8 // lv.parts)

    def planes(i):
        x = lv.off + start + width * i
        for r in lv.tiles(halo):
            now = Batch()
            sums, cells = fine_sum(lv, now, v_ref, w, x, width, r)
            for j in range(width):
                for p in range(lv.parts):
                    value = keep * cells[j][p] + step * (
                        now.get(inv, p, x, j, r) * (now.get(b_ref, p, x, j, r) + sums[j][p])
                    )
                    if old_ref is not None:
                        value = value - old * now.get(old_ref, p, x, j, r)
                    now.put(out_ref, p, x, j, r, value)
            now.flush()

    loop(count // width, 1, planes)


def fine_restrict(lv, b_ref, w, v_ref, tmp_ref, halo=0):
    diag = w[4]
    parts = lv.parts
    count = lv.n + 2 * halo
    width = 2 * turns(count // 2, 4 // parts)

    def planes(i):
        x = lv.off - halo + width * i
        for r in lv.tiles(halo):
            now = Batch()
            sums, cells = fine_sum(lv, now, v_ref, w, x, width, r)
            for pair in range(width // 2):
                total = [None] * max(parts // 2, 1)
                for j in (2 * pair, 2 * pair + 1):
                    for p in range(parts):
                        res = (now.get(b_ref, p, x, j, r) + sums[j][p]) - now.get(
                            diag, p, x, j, r
                        ) * cells[j][p]
                        q = p // 2
                        total[q] = res if total[q] is None else total[q] + res
                for q, value in enumerate(total):
                    tmp_ref[q, width // 2 * i + pair, pl.ds(r - ROW0 + halo, 8), :] = value

    loop(count // width, 1, planes)


def fold_x(lv, k_ref, tmp_ref):
    def pair(i):
        for r in lv.tiles(0):
            for q in range(max(lv.parts // 2, 1)):
                total = None
                for p in range(lv.parts):
                    if p // 2 == q:
                        for k in range(2):
                            value = k_ref[p, lv.off + 2 * i + k, pl.ds(r, 8), :]
                            total = value if total is None else total + value
                tmp_ref[q, i, pl.ds(r - ROW0, 8), :] = total

    loop(lv.n // 2, 1, pair)


def fold_y(lv, tmp_ref, out_ref, off, scale, halo=0):
    half = lv.n // 2 + halo
    for q in range(lv.parts // 2):
        sums = []
        for i in range(half):
            even = tmp_ref[q, i, pl.ds(0, half, stride=2), :]
            odd = tmp_ref[q, i, pl.ds(1, half, stride=2), :]
            sums.append(scale * (even + odd))
        for i in range(half):
            out_ref[q, off - halo // 2 + i, pl.ds(ROW0 - halo // 2, half), :] = sums[i]


def fold_z(tmp_ref, left_ref, matrix, scale):
    for i in range(2):
        for j in range(2):
            row = tmp_ref[0, i, pl.ds(2 * j, 1), :] + tmp_ref[0, i, pl.ds(2 * j + 1, 1), :]
            left_ref[pl.ds(i, 1), pl.ds(LANES * j, LANES)] = scale * row
    return exact_dot(left_ref[...], matrix)


def fine_correct(lv, next_lv, e_ref, s_ref, t_ref, halo):
    next_halo = -(-halo // 2)
    row_lo = ROW0 - next_halo
    rows = next_lv.n + 2 * next_halo
    starts = [row_lo + 8 * t for t in range(-(-rows // 8))]
    if len(starts) == 2:
        starts = [4, 12]

    def plane(i):
        big = next_lv.off - next_halo + i
        for q in range(next_lv.parts):
            for r in starts:
                e = e_ref[q, big, pl.ds(r, 8), :]
                base = 2 * (r - ROW0) + ROW0
                held = []
                for p in (2 * q, 2 * q + 1):
                    for k in range(2):
                        x = lv.off + 2 * (i - next_halo) + k
                        for c in range(2):
                            at = (p, x, pl.ds(base + c, 8, stride=2), slice(None))
                            held.append((at, s_ref[at] + e))
                for at, value in held:
                    t_ref[at] = value

    loop(next_lv.n + 2 * next_halo, 1, plane)


def coarse_rolls(lv, ref, first, count, r):
    return [roll(ref[first - 1 + i, pl.ds(r, 8), :], LANES // 2) for i in range(count + 2)]


def coarse_beside(lv, ref, first, count, r):
    out = []
    low = lane_iota() < LANES // 2
    turned = coarse_rolls(lv, ref, first, count, r) if lv.split else None
    for i in range(count):
        y = first + i
        v = ref[y, pl.ds(r, 8), :]
        xm, xp = ref[y, pl.ds(r - 1, 8), :], ref[y, pl.ds(r + 1, 8), :]
        if lv.split:
            ym = jnp.where(low, turned[i], turned[i + 1])
            yp = jnp.where(low, turned[i + 1], turned[i + 2])
        else:
            ym, yp = ref[y - 1, pl.ds(r, 8), :], ref[y + 1, pl.ds(r, 8), :]
        out.append((v, xm, xp, ym, yp, roll(v, lv.step), roll(v, -lv.step)))
    return out


def coarse_setup(lv, k_ref, w):
    lane = lane_iota() % (LANES // 2)
    bottom, top = lane < lv.step, lane >= LANES // 2 - lv.step
    group = 16 if lv.split else 8

    def planes(i):
        first = 1 + group * i
        for r in lv.tiles:
            for j, (k, xm, xp, ym, yp, zm, zp) in enumerate(
                coarse_beside(lv, k_ref, first, group, r)
            ):
                y = first + j
                zm, zp = jnp.where(bottom, 0.0, zm), jnp.where(top, 0.0, zp)
                w[0][0, y, pl.ds(r, 8), :] = 0.5 * (k + xm)
                w[0][1, y, pl.ds(r, 8), :] = 0.5 * (k + xp)
                w[0][2, y, pl.ds(r, 8), :] = 0.5 * (k + ym)
                w[0][3, y, pl.ds(r, 8), :] = 0.5 * (k + yp)
                w[0][4, y, pl.ds(r, 8), :] = jnp.where(bottom, 0.0, 0.5 * (k + zm))
                w[0][5, y, pl.ds(r, 8), :] = jnp.where(top, 0.0, 0.5 * (k + zp))
                d = 3.0 * k + 0.5 * (((xm + xp) + (ym + yp)) + (zm + zp))
                w[0][6, y, pl.ds(r, 8), :] = d
                w[0][7, y, pl.ds(r, 8), :] = 1.0 / d

    loop(lv.planes // group, 1, planes)


def coarse_apply(lv, w, v_ref, out_ref, fn):
    group = 16 if lv.split else 8

    def planes(i):
        first = 1 + group * i
        held = []
        for r in lv.tiles:
            for j, beside in enumerate(coarse_beside(lv, v_ref, first, group, r)):
                y = first + j
                terms = [w[0][f, y, pl.ds(r, 8), :] * beside[1 + f] for f in range(6)]
                total = ((terms[0] + terms[1]) + (terms[2] + terms[3])) + (terms[4] + terms[5])
                held.append((y, r, fn(y, r, beside[0], total)))
        for y, r, value in held:
            out_ref[y, pl.ds(r, 8), :] = value

    loop(lv.planes // group, 1, planes)


def coarse_first(lv, b_ref, w, out_ref):
    def plane(i):
        for r in lv.tiles:
            at = (1 + i, pl.ds(r, 8), slice(None))
            out_ref[at] = FIRST * (w[0][7, 1 + i, pl.ds(r, 8), :] * b_ref[at])

    loop(lv.planes, 4, plane)


def coarse_step(lv, b_ref, w, v_ref, old_ref, out_ref, keep, old, step):
    def tile(y, r, v, total):
        at = (y, pl.ds(r, 8), slice(None))
        value = keep * v + step * (w[0][7, y, pl.ds(r, 8), :] * (b_ref[at] + total))
        if old_ref is not None:
            value = value - old * old_ref[at]
        return value

    coarse_apply(lv, w, v_ref, out_ref, tile)


def coarse_residual(lv, b_ref, w, v_ref, out_ref):
    def tile(y, r, v, total):
        at = (y, pl.ds(r, 8), slice(None))
        return (b_ref[at] + total) - w[0][6, y, pl.ds(r, 8), :] * v

    coarse_apply(lv, w, v_ref, out_ref, tile)


def coarse_fold(lv, next_lv, ref, out_ref, scale):
    lane = lane_iota()
    even = (lane // lv.step) % 2 == 0
    joined = lv.planes // next_lv.planes

    group = 8

    def planes(i):
        totals = []
        for k in range(group):
            for r in next_lv.tiles:
                base = ROW0 + 2 * (r - ROW0)
                y = 1 + joined * (group * i + k)
                terms = [
                    ref[y + j, pl.ds(base + c, 8, stride=2), :]
                    for j in range(joined)
                    for c in range(2)
                ]
                total = terms[0] + terms[1]
                if joined == 2:
                    total = total + (terms[2] + terms[3])
                totals.append(total)
        if lv.split:
            totals = [total + roll(total, LANES // 2) for total in totals]
        totals = [
            scale * (total + jnp.where(even, roll(total, -lv.step), roll(total, lv.step)))
            for total in totals
        ]
        for k in range(group):
            for j, r in enumerate(next_lv.tiles):
                out_ref[1 + group * i + k, pl.ds(r, 8), :] = totals[k * len(next_lv.tiles) + j]

    loop(next_lv.planes // group, 1, planes)


def coarse_correct(lv, next_lv, e_ref, s_ref, t_ref):
    joined = lv.planes // next_lv.planes

    def plane(i):
        for r in next_lv.tiles:
            e = e_ref[1 + i, pl.ds(r, 8), :]
            base = ROW0 + 2 * (r - ROW0)
            held = []
            for j in range(joined):
                for c in range(2):
                    at = (1 + joined * i + j, pl.ds(base + c, 8, stride=2), slice(None))
                    held.append((at, s_ref[at] + e))
            for at, value in held:
                t_ref[at] = value

    loop(next_lv.planes, 4, plane)


def zero_margin(lv, ref):
    zero = jnp.zeros((8, LANES), F32)
    for y in (0, lv.planes + 1):
        for r in lv.tiles:
            ref[y, pl.ds(r, 8), :] = zero

    def plane(y):
        ref[y, pl.ds(0, 8), :] = zero
        ref[y, pl.ds(ROW0 + lv.n, 8), :] = zero

    loop(lv.planes + 2, 1, plane)


class Links:
    def __init__(self, send, recv):
        self.send, self.recv, self.used = send, recv, 0

    def group(self):
        index = self.used
        self.used += 1

        def copy(src, dst, device):
            return pltpu.make_async_remote_copy(
                src_ref=src,
                dst_ref=dst,
                send_sem=self.send.at[index],
                recv_sem=self.recv.at[index],
                device_id=device,
                device_id_type=MESH,
            )

        return copy


class Halo:
    def __init__(self, place, links, groups):
        gx, gy, nx, ny = place
        self.copies, self.waits = [], []
        for copies, whole in groups:
            copy = links.group()
            for (dx, dy), src, dst in copies:
                device = (lax.rem(gx + dx + nx, nx), lax.rem(gy + dy + ny, ny))
                self.copies.append(copy(src, dst, device))
            self.waits.append(copy(whole, whole, device))

    def start(self):
        for copy in self.copies:
            copy.start()

    def wait_recv(self):
        for wait in self.waits:
            wait.wait_recv()

    def wait_send(self):
        for wait in self.waits:
            wait.wait_send()


def there(place, dx, dy):
    gx, gy, nx, ny = place
    ok = None
    for at, by, size in ((gx, dx, nx), (gy, dy, ny)):
        if by:
            test = at + by < size if by > 0 else at + by >= 0
            ok = test if ok is None else jnp.logical_and(ok, test)
    return True if ok is None else ok


class Rim:
    def __init__(self, lv, halo, corner, refs):
        self.lv, self.halo, self.corner = lv, halo, corner
        self.send_x, self.send_y, self.recv_x, self.recv_y = refs

    @staticmethod
    def scratch(lv, halo, corner):
        n, parts = lv.n, lv.parts
        return [
            pltpu.VMEM((2, parts, halo, n, LANES), F32),
            pltpu.VMEM((2, parts, n, halo, LANES), F32),
            pltpu.VMEM((2, parts, halo, n, LANES), F32),
            pltpu.VMEM((2, parts, n + 2 * corner, halo, LANES), F32),
        ]

    def pack(self, ref):
        lv, h = self.lv, self.halo
        for side, start in ((0, lv.off), (1, lv.off + lv.n - h)):
            for p in range(lv.parts):
                for i in range(h):
                    self.send_x[side, p, i] = ref[p, start + i, pl.ds(ROW0, lv.n), :]

        def plane(i):
            for p in range(lv.parts):
                self.send_y[0, p, i] = ref[p, lv.off + i, pl.ds(ROW0, h), :]
                self.send_y[1, p, i] = ref[p, lv.off + i, pl.ds(ROW0 + lv.n - h, h), :]

        loop(lv.n, 2, plane)

    def exchange(self, place, links):
        c, n = self.corner, self.lv.n
        faces, others = [], []
        for dx, dy in NEIGHBOURS:
            if dy == 0:
                src = self.send_x.at[1 if dx > 0 else 0]
                faces.append(((dx, dy), src, self.recv_x.at[0 if dx > 0 else 1]))
                continue
            src = self.send_y.at[1 if dy > 0 else 0]
            dst = self.recv_y.at[0 if dy > 0 else 1]
            if dx == 0:
                dst = dst.at[:, c : c + n]
            elif dx > 0:
                src, dst = src.at[:, n - c : n], dst.at[:, 0:c]
            else:
                src, dst = src.at[:, 0:c], dst.at[:, c + n : n + 2 * c]
            others.append(((dx, dy), src, dst))
        return Halo(place, links, [(others, self.recv_y), (faces, self.recv_x)])

    def unpack(self, ref, place):
        lv, h, c, n = self.lv, self.halo, self.corner, self.lv.n
        for side, start, dx in ((0, lv.off - h, -1), (1, lv.off + n, 1)):
            ok = there(place, dx, 0)
            for p in range(lv.parts):
                for i in range(h):
                    value = self.recv_x[side, p, i]
                    ref[p, start + i, pl.ds(ROW0, n), :] = jnp.where(ok, value, 0.0)

        gx, gy, nx, ny = place

        def plane(i):
            cell = gx * n + (i - c)
            in_x = jnp.logical_and(cell >= 0, cell < nx * n)
            for side, row, dy in ((0, ROW0 - h, -1), (1, ROW0 + n, 1)):
                ok = jnp.logical_and(in_x, there(place, 0, dy))
                for p in range(lv.parts):
                    value = self.recv_y[side, p, i]
                    ref[p, lv.off - c + i, pl.ds(row, h), :] = jnp.where(ok, value, 0.0)

        loop(n + 2 * c, 2, plane)


class Blocks:
    def __init__(self, lv, refs):
        self.lv = lv
        self.send, self.recv = refs

    @staticmethod
    def scratch(lv):
        n = lv.n
        return [pltpu.VMEM((n, n, LANES), F32), pltpu.VMEM((8, n, n, LANES), F32)]

    def pack(self, ref):
        lv = self.lv
        for i in range(lv.n):
            self.send[i] = ref[0, lv.off + i, pl.ds(ROW0, lv.n), :]

    def exchange(self, place, links):
        n = self.lv.n
        copies = []
        for dx, dy in NEIGHBOURS:
            slot = (1 + dy) * 3 + 1 + dx
            slot -= 1 if slot > 4 else 0
            copies.append(((dx, dy), self.send, self.recv.at[slot]))
        return Halo(place, links, [(copies, self.recv)])

    def unpack(self, ref, place):
        lv, n = self.lv, self.lv.n
        for dx, dy in NEIGHBOURS:
            slot = (1 + dy) * 3 + 1 + dx
            slot -= 1 if slot > 4 else 0
            ok = there(place, -dx, -dy)
            for k in range(n):
                ref[0, lv.off - n * dx + k, pl.ds(ROW0 - n * dy, n), :] = jnp.where(
                    ok, self.recv[slot, k], 0.0
                )


class Gather:
    def __init__(self, place, links, piece_ref, whole_ref):
        gx, gy, nx, ny = place
        self.place = place
        self.piece, self.whole = piece_ref, whole_ref
        order_x = sorted(range(1, nx), key=lambda d: -min(d // 2, (nx - d) // 2))
        order_y = range(1, ny)
        mine = piece_ref.at[gx]
        copy = links.group()
        self.along_x = [copy(mine, mine, (lax.rem(gx + d, nx), gy)) for d in order_x]
        rest = piece_ref.at[0 : nx - 1]
        self.wait_x = copy(rest, rest, (lax.rem(gx + 1, nx), gy))
        slab = whole_ref.at[1 + gy, pl.ds(ROW0, 2 * nx), :]
        copy = links.group()
        self.along_y = [copy(slab, slab, (gx, lax.rem(gy + d, ny))) for d in order_y]
        rest = whole_ref.at[1:ny, pl.ds(ROW0, 2 * nx), :]
        self.wait_y = copy(rest, rest, (gx, lax.rem(gy + 1, ny)))

    def start_x(self, value):
        gx = self.place[0]
        self.piece[gx] = value
        for copy in self.along_x:
            copy.start()

    def start_y(self):
        gx, gy, nx, ny = self.place
        self.wait_x.wait_recv()
        for i in range(nx):
            self.whole[1 + gy, pl.ds(ROW0 + 2 * i, 2), :] = self.piece[i]
        for copy in self.along_y:
            copy.start()

    def finish(self):
        self.wait_y.wait_recv()

    def wait_send(self):
        self.wait_x.wait_send()
        self.wait_y.wait_send()


RIMS = {
    "rk0": (L0, 3, 2),
    "rb0": (L0, 2, 1),
    "rs0": (L0, 2, 1),
    "rk1": (L1, 7, 7),
    "rb1": (L1, 6, 5),
}


def scratch_shapes(nx, ny):
    l3, l4, l5 = coarse_levels(nx, ny)
    shapes = {}
    for name in ("raw_k", "raw_b"):
        shapes[name] = pltpu.VMEM((L0.n, L0.n, L0.parts * LANES), F32)
    shapes["perm"] = pltpu.VMEM((512, 512), BF16)
    shapes["left"] = pltpu.VMEM((8, 2 * LANES), F32)
    for i, lv in enumerate((L0, L1, L2)):
        for name in ("k", "b", "wx", "wy", "inv", "diag", "x", "s", "t"):
            shapes[name + str(i)] = pltpu.VMEM(lv.shape, F32)
        shapes["wz" + str(i)] = pltpu.VMEM((lv.parts + 1,) + lv.shape[1:], F32)
        shapes["tmp" + str(i)] = pltpu.VMEM((max(lv.parts // 2, 1), 8, 16, LANES), F32)
    shapes["e2"] = pltpu.VMEM((6, L2.rows, LANES), F32)
    for i, lv in ((3, l3), (4, l4), (5, l5)):
        for name in ("k", "b", "x", "s", "t"):
            shapes[name + str(i)] = pltpu.VMEM(lv.shape, F32)
        shapes["w" + str(i)] = pltpu.VMEM((8,) + lv.shape, F32)
    for name, (lv, halo, corner) in RIMS.items():
        for j, shape in enumerate(Rim.scratch(lv, halo, corner)):
            shapes[name + "_" + str(j)] = shape
    for name in ("rk2", "rb2", "rs2"):
        for j, shape in enumerate(Blocks.scratch(L2)):
            shapes[name + "_" + str(j)] = shape
    for name in ("pk3", "pb3"):
        shapes[name] = pltpu.VMEM((nx, 2, LANES), F32)
    copies = 5 * 2 + 3 + 2 * 2
    shapes["send"] = pltpu.SemaphoreType.DMA((copies,))
    shapes["recv"] = pltpu.SemaphoreType.DMA((copies,))
    shapes["local"] = pltpu.SemaphoreType.DMA((4,))
    return shapes


def coarse_levels(nx, ny):
    return (
        Coarse(ny, 2 * nx, 1, True),
        Coarse(ny, nx, 2, False),
        Coarse(ny // 2, nx // 2, 4, False),
    )


def kernel(nx, ny, names, b_in, k_in, out_ref, *refs):
    m = dict(zip(names, refs))
    gx, gy = lax.axis_index("gx"), lax.axis_index("gy")
    place = (gx, gy, nx, ny)
    l3, l4, l5 = coarse_levels(nx, ny)
    links = Links(m["send"], m["recv"])

    def pair(name, cls, *args):
        refs = [m[key] for key in names if key.startswith(name + "_")]
        return cls(*args, refs)

    rk0, rb0, rs0, rk1, rb1 = (pair(name, Rim, *RIMS[name]) for name in RIMS)
    rk2, rb2, rs2 = (pair(name, Blocks, L2) for name in ("rk2", "rb2", "rs2"))
    hk0, hb0, hs0, hk1, hb1, hk2, hb2, hs2 = (
        rim.exchange(place, links) for rim in (rk0, rb0, rs0, rk1, rb1, rk2, rb2, rs2)
    )
    gk3 = Gather(place, links, m["pk3"], m["k3"])
    gb3 = Gather(place, links, m["pb3"], m["b3"])

    load_k = pltpu.make_async_copy(k_in, m["raw_k"], m["local"].at[0])
    load_b = pltpu.make_async_copy(b_in, m["raw_b"], m["local"].at[1])
    load_k.start()
    load_b.start()

    barrier = pltpu.get_barrier_semaphore()
    peers = [(dx, dy) for dx, dy in NEIGHBOURS]
    peers += [(d, 0) for d in range(2, nx - 1)] + [(0, d) for d in range(2, ny - 1)]
    for dx, dy in peers:
        pl.semaphore_signal(
            barrier,
            inc=1,
            device_id=(lax.rem(gx + dx + nx, nx), lax.rem(gy + dy + ny, ny)),
            device_id_type=MESH,
        )

    def fill(i):
        start = pl.multiple_of(i * 64, 64)
        m["perm"][pl.ds(start, 64), :] = one(
            64, 512, lambda at, to: at + start == 4 * (to % LANES) + to // LANES
        )

    loop(8, 1, fill)
    m["left"][...] = jnp.zeros_like(m["left"])
    fold = one(
        2 * LANES,
        LANES,
        lambda at, to: jnp.logical_and(at // LANES == to // 64, (at % LANES) // 2 == to % 64),
    )
    unfold = one(
        LANES,
        2 * LANES,
        lambda at, to: jnp.logical_and(to // LANES == at // 64, (to % LANES) // 2 == at % 64),
    )

    def reorder(raw, ref):
        half = L0.n // 2
        for c in range(2):
            value = raw[c * half : (c + 1) * half].reshape(half * L0.n, 512)
            moved = exact_dot(value, m["perm"][...])
            for p in range(L0.parts):
                ref[p, pl.ds(L0.off + c * half, half), pl.ds(ROW0, L0.n), :] = moved[
                    :, p * LANES : (p + 1) * LANES
                ].reshape(half, L0.n, LANES)

    load_k.wait()
    reorder(m["raw_k"], m["k0"])
    rk0.pack(m["k0"])
    pl.semaphore_wait(barrier, len(peers))
    hk0.start()
    load_b.wait()
    reorder(m["raw_b"], m["b0"])
    rb0.pack(m["b0"])
    hb0.start()

    fold_x(L0, m["k0"], m["tmp0"])
    fold_y(L0, m["tmp0"], m["k1"], L1.off, 0.125)
    fold_x(L1, m["k1"], m["tmp1"])
    fold_y(L1, m["tmp1"], m["k2"], L2.off, 0.125)
    rk2.pack(m["k2"])
    hk2.start()
    fold_x(L2, m["k2"], m["tmp2"])
    gk3.start_x(fold_z(m["tmp2"], m["left"], fold, 0.125)[0:2])
    for lv, i in ((l3, 3), (l4, 4), (l5, 5)):
        for name in ("k", "x", "s", "t"):
            zero_margin(lv, m[name + str(i)])

    weights = [
        tuple(m[name + str(i)] for name in ("wx", "wy", "wz", "inv", "diag")) for i in range(3)
    ]
    sizes = [(nx * lv.n, ny * lv.n) for lv in (L0, L1, L2)]
    w3, w4, w5 = (m["w3"],), (m["w4"],), (m["w5"],)

    hk0.wait_recv()
    rk1.pack(m["k1"])
    hk1.start()
    rk0.unpack(m["k0"], place)
    fine_setup(L0, m["k0"], weights[0], gx, gy, *sizes[0])
    hb0.wait_recv()
    rb0.unpack(m["b0"], place)
    fine_first(L0, m["b0"], weights[0], m["x0"], 2)
    fine_step(L0, m["b0"], weights[0], m["x0"], None, m["s0"], 1, KEEP, OLD, STEP)
    fine_restrict(L0, m["b0"], weights[0], m["s0"], m["tmp0"])
    fold_y(L0, m["tmp0"], m["b1"], L1.off, 0.5)
    rb1.pack(m["b1"])
    hb1.start()
    rs0.pack(m["s0"])
    hs0.start()

    gk3.start_y()
    hk1.wait_recv()
    rk1.unpack(m["k1"], place)
    fine_setup(L1, m["k1"], weights[1], gx, gy, *sizes[1])
    hk2.wait_recv()
    rk2.unpack(m["k2"], place)
    fine_setup(L2, m["k2"], weights[2], gx, gy, *sizes[2])

    hb1.wait_recv()
    rb1.unpack(m["b1"], place)
    fine_first(L1, m["b1"], weights[1], m["x1"], 6)
    fine_step(L1, m["b1"], weights[1], m["x1"], None, m["s1"], 5, KEEP, OLD, STEP)
    fine_restrict(L1, m["b1"], weights[1], m["s1"], m["tmp1"], 4)
    fold_y(L1, m["tmp1"], m["b2"], L2.off, 0.5, 4)

    fine_first(L2, m["b2"], weights[2], m["x2"], 2)
    fine_step(L2, m["b2"], weights[2], m["x2"], None, m["s2"], 1, KEEP, OLD, STEP)
    fine_restrict(L2, m["b2"], weights[2], m["s2"], m["tmp2"])
    gb3.start_x(fold_z(m["tmp2"], m["left"], fold, 0.5)[0:2])
    rb2.pack(m["b2"])
    hb2.start()
    rs2.pack(m["s2"])
    hs2.start()

    gk3.finish()
    coarse_setup(l3, m["k3"], w3)
    gb3.start_y()
    coarse_fold(l3, l4, m["k3"], m["k4"], 0.125)
    coarse_setup(l4, m["k4"], w4)
    coarse_fold(l4, l5, m["k4"], m["k5"], 0.125)
    coarse_setup(l5, m["k5"], w5)
    for part in (hs0, hb2, hs2):
        part.wait_recv()
        part.wait_send()
    rs0.unpack(m["s0"], place)
    rb2.unpack(m["b2"], place)
    rs2.unpack(m["s2"], place)
    gb3.finish()

    coarse_first(l3, m["b3"], w3, m["x3"])
    coarse_step(l3, m["b3"], w3, m["x3"], None, m["s3"], KEEP, OLD, STEP)
    coarse_residual(l3, m["b3"], w3, m["s3"], m["t3"])
    coarse_fold(l3, l4, m["t3"], m["b4"], 0.5)
    coarse_first(l4, m["b4"], w4, m["x4"])
    coarse_step(l4, m["b4"], w4, m["x4"], None, m["s4"], KEEP, OLD, STEP)
    coarse_residual(l4, m["b4"], w4, m["s4"], m["t4"])
    coarse_fold(l4, l5, m["t4"], m["b5"], 0.5)
    coarse_first(l5, m["b5"], w5, m["x5"])
    now, old, spare = m["x5"], None, [m["s5"], m["t5"]]
    rho = RHO0
    for _ in range(COARSE_ITERS - 1):
        rho_new = 1.0 / (2.0 * SIGMA - rho)
        keep = 1.0 + rho_new * rho - 2.0 * rho_new / RADIUS
        out = spare.pop(0)
        coarse_step(l5, m["b5"], w5, now, old, out, keep, rho_new * rho, 2.0 * rho_new / RADIUS)
        if old is not None:
            spare.append(old)
        now, old, rho = out, now, rho_new
    coarse_correct(l4, l5, now, m["s4"], m["t4"])
    coarse_step(l4, m["b4"], w4, m["t4"], None, m["x4"], 1.0 - FIRST, 0.0, FIRST)
    coarse_step(l4, m["b4"], w4, m["x4"], m["t4"], m["s4"], KEEP, OLD, STEP)
    coarse_correct(l3, l4, m["s4"], m["s3"], m["t3"])
    coarse_step(l3, m["b3"], w3, m["t3"], None, m["x3"], 1.0 - FIRST, 0.0, FIRST)
    coarse_step(l3, m["b3"], w3, m["x3"], m["t3"], m["s3"], KEEP, OLD, STEP)

    near = jnp.concatenate(
        [m["s3"][gy + d, pl.ds(2 * gx + ROW0 - 2, 8), :] for d in range(3)], axis=0
    )
    wide = exact_dot(near, unfold)
    for d in range(3):
        for i in range(6):
            for a in range(2):
                row = wide[8 * d + i : 8 * d + i + 1, a * LANES : (a + 1) * LANES]
                m["e2"][i, pl.ds(ROW0 - 4 + 4 * d + 2 * a, 2), :] = jnp.broadcast_to(
                    row, (2, LANES)
                )
    for i in range(6):
        for k in range(2):
            x = L2.off - 4 + 2 * i + k
            for r in L2.tiles(4):
                m["t2"][0, x, pl.ds(r, 8), :] = (
                    m["s2"][0, x, pl.ds(r, 8), :] + m["e2"][i, pl.ds(r, 8), :]
                )
    fine_step(L2, m["b2"], weights[2], m["t2"], None, m["x2"], 3, 1.0 - FIRST, 0.0, FIRST)
    fine_step(L2, m["b2"], weights[2], m["x2"], m["t2"], m["s2"], 2, KEEP, OLD, STEP)

    fine_correct(L1, L2, m["s2"], m["s1"], m["t1"], 3)
    fine_step(L1, m["b1"], weights[1], m["t1"], None, m["x1"], 2, 1.0 - FIRST, 0.0, FIRST)
    fine_step(L1, m["b1"], weights[1], m["x1"], m["t1"], m["s1"], 1, KEEP, OLD, STEP)

    fine_correct(L0, L1, m["s1"], m["s0"], m["t0"], 2)
    fine_step(L0, m["b0"], weights[0], m["t0"], None, m["x0"], 1, 1.0 - FIRST, 0.0, FIRST)
    half = L0.n // 2
    stores = []
    for c in range(2):
        fine_step(
            L0, m["b0"], weights[0], m["x0"], m["t0"], m["s0"], 0, KEEP, OLD, STEP, c * half, half
        )
        stores.append(
            pltpu.make_async_copy(
                m["s0"].at[:, pl.ds(L0.off + c * half, half), pl.ds(ROW0, L0.n), :],
                out_ref.at[:, pl.ds(c * half, half)],
                m["local"].at[2 + c],
            )
        )
        stores[c].start()
    for part in (hk0, hb0, hk1, hb1, hk2, gk3, gb3):
        part.wait_send()
    for store in stores:
        store.wait()


CHUNKS = 1


def finish(parts_ref, out_ref, held, back, out, load_sem, store_sem):
    n = L0.n
    size = n // CHUNKS

    def chunk(c):
        return pl.ds(c * size, size)

    loads = [
        pltpu.make_async_copy(parts_ref.at[:, chunk(c)], held.at[:, chunk(c)], load_sem.at[c])
        for c in range(CHUNKS)
    ]
    stores = [
        pltpu.make_async_copy(out.at[chunk(c)], out_ref.at[chunk(c)], store_sem.at[c])
        for c in range(CHUNKS)
    ]
    for load in loads:
        load.start()

    def fill(i):
        start = pl.multiple_of(i * 64, 64)
        back[pl.ds(start, 64), :] = one(
            64, 512, lambda at, to: to == 4 * ((at + start) % LANES) + (at + start) // LANES
        )

    loop(8, 1, fill)
    for c in range(CHUNKS):
        loads[c].wait()
        value = jnp.concatenate(
            [held[p, chunk(c)].reshape(size * n, LANES) for p in range(L0.parts)], axis=1
        )
        out[chunk(c)] = exact_dot(value, back[...]).reshape(size, n, 512)
        stores[c].start()
    for store in stores:
        store.wait()


def solution(mesh):
    nx, ny = mesh.shape["gx"], mesh.shape["gy"]
    shapes = scratch_shapes(nx, ny)

    def body(right_side, coefficient):
        parts = pl.pallas_call(
            functools.partial(kernel, nx, ny, list(shapes)),
            out_shape=jax.ShapeDtypeStruct((L0.parts, L0.n, L0.n, LANES), F32),
            in_specs=[pl.BlockSpec(memory_space=pl.ANY)] * 2,
            out_specs=pl.BlockSpec(memory_space=pl.ANY),
            scratch_shapes=list(shapes.values()),
            compiler_params=pltpu.CompilerParams(
                collective_id=0, has_side_effects=True, vmem_limit_bytes=56 * 1024 * 1024
            ),
        )(right_side, coefficient)
        return pl.pallas_call(
            finish,
            out_shape=jax.ShapeDtypeStruct(right_side.shape, F32),
            in_specs=[pl.BlockSpec(memory_space=pl.ANY)],
            out_specs=pl.BlockSpec(memory_space=pl.ANY),
            scratch_shapes=[
                pltpu.VMEM((L0.parts, L0.n, L0.n, LANES), F32),
                pltpu.VMEM((512, 512), BF16),
                pltpu.VMEM((L0.n, L0.n, 512), F32),
                pltpu.SemaphoreType.DMA((CHUNKS,)),
                pltpu.SemaphoreType.DMA((CHUNKS,)),
            ],
            compiler_params=pltpu.CompilerParams(vmem_limit_bytes=60 * 1024 * 1024),
        )(parts)

    return jax.shard_map(
        body,
        mesh=mesh,
        in_specs=(P("gx", "gy", None), P("gx", "gy", None)),
        out_specs=P("gx", "gy", None),
        check_vma=False,
    )
```

```python
import functools

import jax
import jax.numpy as jnp
from jax import lax
from jax.experimental import pallas as pl
from jax.experimental.pallas import tpu as pltpu
from jax.sharding import PartitionSpec as P

MESH = pl.DeviceIdType.MESH
F32 = jnp.float32
BF16 = jnp.bfloat16

CENTRE = 1.15
RADIUS = 0.85
COARSE_ITERS = 6
SIGMA = CENTRE / RADIUS
RHO0 = 1.0 / SIGMA
RHO1 = 1.0 / (2.0 * SIGMA - RHO0)
KEEP = 1.0 + RHO1 * RHO0 - 2.0 * RHO1 / RADIUS
OLD = RHO1 * RHO0
STEP = 2.0 * RHO1 / RADIUS
FIRST = 1.0 / CENTRE

NEIGHBOURS = [(dx, dy) for dx in (-1, 0, 1) for dy in (-1, 0, 1) if (dx, dy) != (0, 0)]
ROW0 = 8
LANES = 128


class Fine:
    def __init__(self, parts, n, off, rows, halo_inv):
        self.parts, self.n, self.off, self.rows, self.halo_inv = parts, n, off, rows, halo_inv
        self.planes = n + 2 * off
        self.shape = (parts, self.planes, rows, LANES)

    def tiles(self, halo):
        low, count = ROW0 - halo, self.n + 2 * halo
        if halo == 0:
            return [low + 8 * t for t in range(-(-count // 8))]
        if count % 8 == 0:
            return [low + 8 * t for t in range(count // 8)]
        tiles = -(-count // 8)
        low = max(1, low - (tiles * 8 - count) // 2)
        return [low + 8 * t for t in range(tiles)]


class Coarse:
    def __init__(self, planes, n, step, split):
        self.planes, self.n, self.step, self.split = planes, n, step, split
        self.shape = (planes + 2, n + 16, LANES)
        self.tiles = [ROW0 + 8 * t for t in range(n // 8)]


L0 = Fine(4, 16, 4, 32, 2)
L1 = Fine(2, 8, 8, 32, 6)
L2 = Fine(1, 4, 5, 24, 3)


def roll(value, by):
    return pltpu.roll(value, by % LANES, 1)


def lane_iota():
    return lax.broadcasted_iota(jnp.int32, (8, LANES), 1)


def loop(count, step, fn):
    assert count % step == 0

    def turn(i, carry):
        for k in range(step):
            fn(i * step + k)
        return carry

    lax.fori_loop(0, count // step, turn, 0)


def turns(count, most):
    return max(d for d in range(1, most + 1) if count % d == 0)


def split3(value):
    high = value.astype(BF16)
    rest = value - high.astype(F32)
    mid = rest.astype(BF16)
    low = (rest - mid.astype(F32)).astype(BF16)
    return high, mid, low


def exact_dot(value, matrix):
    rows = value.shape[0]
    moved = jnp.dot(
        jnp.concatenate(split3(value), axis=0), matrix, preferred_element_type=F32
    )
    return (moved[:rows] + moved[rows : 2 * rows]) + moved[2 * rows :]


def one(rows, cols, test):
    at = lax.broadcasted_iota(jnp.int32, (rows, cols), 0)
    to = lax.broadcasted_iota(jnp.int32, (rows, cols), 1)
    return jnp.where(test(at, to), 1.0, 0.0).astype(BF16)


class Batch:
    def __init__(self):
        self.seen, self.held = {}, []

    def get(self, ref, p, x, dx, r):
        key = (id(ref), p, dx, r)
        if key not in self.seen:
            self.seen[key] = ref[p, x + dx, pl.ds(r, 8), :]
        return self.seen[key]

    def put(self, ref, p, x, dx, r, value):
        self.held.append((ref, p, x, dx, r, value))

    def flush(self):
        for ref, p, x, dx, r, value in self.held:
            ref[p, x + dx, pl.ds(r, 8), :] = value
        self.held = []


def fine_setup(lv, k_ref, w, gx, gy, size_x, size_y):
    wx, wy, wz, inv, diag = w
    h = lv.halo_inv
    lane = lane_iota()
    row = lax.broadcasted_iota(jnp.int32, (8, LANES), 0)
    parts = lv.parts
    start, count, tiles = -h, lv.n + 2 * h + 1, lv.tiles(h)
    width = turns(count, 12 // parts)

    def planes(i):
        x = lv.off + start + width * i
        for r in tiles:
            now = Batch()
            gy_cell = gy * lv.n + (r - ROW0) + row
            in_y = jnp.logical_and(gy_cell >= 0, gy_cell < size_y)
            cells = [[now.get(k_ref, p, x, j, r) for p in range(parts)] for j in range(width)]
            below = [roll(c[parts - 1], 1) for c in cells]
            above = [roll(c[0], -1) for c in cells]
            for j in range(width):
                gx_cell = gx * lv.n + (width * i + j + start)
                inside = jnp.logical_and(in_y, jnp.logical_and(gx_cell >= 0, gx_cell < size_x))
                first = jnp.where(lane == 0, 0.0, below[j])
                last = jnp.where(lane == LANES - 1, 0.0, above[j])
                for p in range(parts):
                    k = cells[j][p]
                    kxm, kxp = now.get(k_ref, p, x, j - 1, r), now.get(k_ref, p, x, j + 1, r)
                    kym, kyp = now.get(k_ref, p, x, j, r - 1), now.get(k_ref, p, x, j, r + 1)
                    kzm = first if p == 0 else cells[j][p - 1]
                    kzp = last if p == parts - 1 else cells[j][p + 1]
                    now.put(wx, p, x, j, r, 0.5 * (k + kxm))
                    now.put(wy, p, x, j, r, 0.5 * (k + kym))
                    down = 0.5 * (k + kzm)
                    if p == 0:
                        down = jnp.where(lane == 0, 0.0, down)
                    now.put(wz, p, x, j, r, down)
                    if p == parts - 1:
                        up = jnp.where(lane == LANES - 1, 0.0, 0.5 * (k + kzp))
                        now.put(wz, parts, x, j, r, up)
                    d = 3.0 * k + 0.5 * (((kxm + kxp) + (kym + kyp)) + (kzm + kzp))
                    now.put(diag, p, x, j, r, d)
                    now.put(inv, p, x, j, r, jnp.where(inside, 1.0 / d, 0.0))
            now.flush()

    loop(count // width, 1, planes)


def fine_sum(lv, now, v_ref, w, x, width, r):
    wx, wy, wz = w[0], w[1], w[2]
    parts = lv.parts
    cells = [[now.get(v_ref, p, x, j, r) for p in range(parts)] for j in range(width)]
    below = [roll(c[parts - 1], 1) for c in cells]
    above = [roll(c[0], -1) for c in cells]
    sums = []
    for j in range(width):
        sums.append([])
        for p in range(parts):
            along_x = now.get(wx, p, x, j, r) * now.get(v_ref, p, x, j - 1, r) + now.get(
                wx, p, x, j + 1, r
            ) * now.get(v_ref, p, x, j + 1, r)
            along_y = now.get(wy, p, x, j, r) * now.get(v_ref, p, x, j, r - 1) + now.get(
                wy, p, x, j, r + 1
            ) * now.get(v_ref, p, x, j, r + 1)
            along_z = now.get(wz, p, x, j, r) * (below[j] if p == 0 else cells[j][p - 1])
            along_z += now.get(wz, p + 1, x, j, r) * (
                above[j] if p == parts - 1 else cells[j][p + 1]
            )
            sums[j].append((along_x + along_y) + along_z)
    return sums, cells


def fine_first(lv, b_ref, w, out_ref, halo):
    inv = w[3]

    def planes(i):
        x = lv.off - halo + 2 * i
        now = Batch()
        for r in lv.tiles(halo):
            for k in range(2):
                for p in range(lv.parts):
                    value = now.get(inv, p, x, k, r) * now.get(b_ref, p, x, k, r)
                    now.put(out_ref, p, x, k, r, FIRST * value)
        now.flush()

    loop((lv.n + 2 * halo) // 2, 1, planes)


def fine_step(
    lv, b_ref, w, v_ref, old_ref, out_ref, halo, keep, old, step, start=None, count=None
):
    inv = w[3]
    if count is None:
        start, count = -halo, lv.n + 2 * halo
    width = turns(count, 16 // lv.parts)

    def planes(i):
        x = lv.off + start + width * i
        for r in lv.tiles(halo):
            now = Batch()
            sums, cells = fine_sum(lv, now, v_ref, w, x, width, r)
            for j in range(width):
                for p in range(lv.parts):
                    value = keep * cells[j][p] + step * (
                        now.get(inv, p, x, j, r) * (now.get(b_ref, p, x, j, r) + sums[j][p])
                    )
                    if old_ref is not None:
                        value = value - old * now.get(old_ref, p, x, j, r)
                    now.put(out_ref, p, x, j, r, value)
            now.flush()

    loop(count // width, 1, planes)


def fine_restrict(lv, b_ref, w, v_ref, tmp_ref, halo=0):
    diag = w[4]
    parts = lv.parts
    count = lv.n + 2 * halo
    width = 2 * turns(count // 2, 4 // parts)

    def planes(i):
        x = lv.off - halo + width * i
        for r in lv.tiles(halo):
            now = Batch()
            sums, cells = fine_sum(lv, now, v_ref, w, x, width, r)
            for pair in range(width // 2):
                total = [None] * max(parts // 2, 1)
                for j in (2 * pair, 2 * pair + 1):
                    for p in range(parts):
                        res = (now.get(b_ref, p, x, j, r) + sums[j][p]) - now.get(
                            diag, p, x, j, r
                        ) * cells[j][p]
                        q = p // 2
                        total[q] = res if total[q] is None else total[q] + res
                for q, value in enumerate(total):
                    tmp_ref[q, width // 2 * i + pair, pl.ds(r - ROW0 + halo, 8), :] = value

    loop(count // width, 1, planes)


def fold_x(lv, k_ref, tmp_ref):
    def pair(i):
        for r in lv.tiles(0):
            for q in range(max(lv.parts // 2, 1)):
                total = None
                for p in range(lv.parts):
                    if p // 2 == q:
                        for k in range(2):
                            value = k_ref[p, lv.off + 2 * i + k, pl.ds(r, 8), :]
                            total = value if total is None else total + value
                tmp_ref[q, i, pl.ds(r - ROW0, 8), :] = total

    loop(lv.n // 2, 1, pair)


def fold_y(lv, tmp_ref, out_ref, off, scale, halo=0):
    half = lv.n // 2 + halo
    for q in range(lv.parts // 2):
        sums = []
        for i in range(half):
            even = tmp_ref[q, i, pl.ds(0, half, stride=2), :]
            odd = tmp_ref[q, i, pl.ds(1, half, stride=2), :]
            sums.append(scale * (even + odd))
        for i in range(half):
            out_ref[q, off - halo // 2 + i, pl.ds(ROW0 - halo // 2, half), :] = sums[i]


def fold_z(tmp_ref, left_ref, matrix, scale):
    for i in range(2):
        for j in range(2):
            row = tmp_ref[0, i, pl.ds(2 * j, 1), :] + tmp_ref[0, i, pl.ds(2 * j + 1, 1), :]
            left_ref[pl.ds(i, 1), pl.ds(LANES * j, LANES)] = scale * row
    return exact_dot(left_ref[...], matrix)


def fine_correct(lv, next_lv, e_ref, s_ref, t_ref, halo):
    next_halo = -(-halo // 2)
    row_lo = ROW0 - next_halo
    rows = next_lv.n + 2 * next_halo
    starts = [row_lo + 8 * t for t in range(-(-rows // 8))]
    if len(starts) == 2:
        starts = [4, 12]

    def plane(i):
        big = next_lv.off - next_halo + i
        for q in range(next_lv.parts):
            for r in starts:
                e = e_ref[q, big, pl.ds(r, 8), :]
                base = 2 * (r - ROW0) + ROW0
                held = []
                for p in (2 * q, 2 * q + 1):
                    for k in range(2):
                        x = lv.off + 2 * (i - next_halo) + k
                        for c in range(2):
                            at = (p, x, pl.ds(base + c, 8, stride=2), slice(None))
                            held.append((at, s_ref[at] + e))
                for at, value in held:
                    t_ref[at] = value

    loop(next_lv.n + 2 * next_halo, 1, plane)


def coarse_rolls(lv, ref, first, count, r):
    return [roll(ref[first - 1 + i, pl.ds(r, 8), :], LANES // 2) for i in range(count + 2)]


def coarse_beside(lv, ref, first, count, r):
    out = []
    low = lane_iota() < LANES // 2
    turned = coarse_rolls(lv, ref, first, count, r) if lv.split else None
    for i in range(count):
        y = first + i
        v = ref[y, pl.ds(r, 8), :]
        xm, xp = ref[y, pl.ds(r - 1, 8), :], ref[y, pl.ds(r + 1, 8), :]
        if lv.split:
            ym = jnp.where(low, turned[i], turned[i + 1])
            yp = jnp.where(low, turned[i + 1], turned[i + 2])
        else:
            ym, yp = ref[y - 1, pl.ds(r, 8), :], ref[y + 1, pl.ds(r, 8), :]
        out.append((v, xm, xp, ym, yp, roll(v, lv.step), roll(v, -lv.step)))
    return out


def coarse_setup(lv, k_ref, w):
    lane = lane_iota() % (LANES // 2)
    bottom, top = lane < lv.step, lane >= LANES // 2 - lv.step
    group = lv.planes

    def planes(i):
        first = 1 + group * i
        for r in lv.tiles:
            for j, (k, xm, xp, ym, yp, zm, zp) in enumerate(
                coarse_beside(lv, k_ref, first, group, r)
            ):
                y = first + j
                zm, zp = jnp.where(bottom, 0.0, zm), jnp.where(top, 0.0, zp)
                w[0][0, y, pl.ds(r, 8), :] = 0.5 * (k + xm)
                w[0][1, y, pl.ds(r, 8), :] = 0.5 * (k + xp)
                w[0][2, y, pl.ds(r, 8), :] = 0.5 * (k + ym)
                w[0][3, y, pl.ds(r, 8), :] = 0.5 * (k + yp)
                w[0][4, y, pl.ds(r, 8), :] = jnp.where(bottom, 0.0, 0.5 * (k + zm))
                w[0][5, y, pl.ds(r, 8), :] = jnp.where(top, 0.0, 0.5 * (k + zp))
                d = 3.0 * k + 0.5 * (((xm + xp) + (ym + yp)) + (zm + zp))
                w[0][6, y, pl.ds(r, 8), :] = d
                w[0][7, y, pl.ds(r, 8), :] = 1.0 / d

    loop(lv.planes // group, 1, planes)


def coarse_apply(lv, w, v_ref, out_ref, fn):
    group = lv.planes

    def planes(i):
        first = 1 + group * i
        held = []
        for r in lv.tiles:
            for j, beside in enumerate(coarse_beside(lv, v_ref, first, group, r)):
                y = first + j
                terms = [w[0][f, y, pl.ds(r, 8), :] * beside[1 + f] for f in range(6)]
                total = ((terms[0] + terms[1]) + (terms[2] + terms[3])) + (terms[4] + terms[5])
                held.append((y, r, fn(y, r, beside[0], total)))
        for y, r, value in held:
            out_ref[y, pl.ds(r, 8), :] = value

    loop(lv.planes // group, 1, planes)


def coarse_first(lv, b_ref, w, out_ref):
    def plane(i):
        for r in lv.tiles:
            at = (1 + i, pl.ds(r, 8), slice(None))
            out_ref[at] = FIRST * (w[0][7, 1 + i, pl.ds(r, 8), :] * b_ref[at])

    loop(lv.planes, 4, plane)


def coarse_step(lv, b_ref, w, v_ref, old_ref, out_ref, keep, old, step):
    def tile(y, r, v, total):
        at = (y, pl.ds(r, 8), slice(None))
        value = keep * v + step * (w[0][7, y, pl.ds(r, 8), :] * (b_ref[at] + total))
        if old_ref is not None:
            value = value - old * old_ref[at]
        return value

    coarse_apply(lv, w, v_ref, out_ref, tile)


def coarse_residual(lv, b_ref, w, v_ref, out_ref):
    def tile(y, r, v, total):
        at = (y, pl.ds(r, 8), slice(None))
        return (b_ref[at] + total) - w[0][6, y, pl.ds(r, 8), :] * v

    coarse_apply(lv, w, v_ref, out_ref, tile)


def coarse_fold(lv, next_lv, ref, out_ref, scale):
    lane = lane_iota()
    even = (lane // lv.step) % 2 == 0
    joined = lv.planes // next_lv.planes

    group = 8

    def planes(i):
        totals = []
        for k in range(group):
            for r in next_lv.tiles:
                base = ROW0 + 2 * (r - ROW0)
                y = 1 + joined * (group * i + k)
                terms = [
                    ref[y + j, pl.ds(base + c, 8, stride=2), :]
                    for j in range(joined)
                    for c in range(2)
                ]
                total = terms[0] + terms[1]
                if joined == 2:
                    total = total + (terms[2] + terms[3])
                totals.append(total)
        if lv.split:
            totals = [total + roll(total, LANES // 2) for total in totals]
        totals = [
            scale * (total + jnp.where(even, roll(total, -lv.step), roll(total, lv.step)))
            for total in totals
        ]
        for k in range(group):
            for j, r in enumerate(next_lv.tiles):
                out_ref[1 + group * i + k, pl.ds(r, 8), :] = totals[k * len(next_lv.tiles) + j]

    loop(next_lv.planes // group, 1, planes)


def coarse_correct(lv, next_lv, e_ref, s_ref, t_ref):
    joined = lv.planes // next_lv.planes

    def plane(i):
        for r in next_lv.tiles:
            e = e_ref[1 + i, pl.ds(r, 8), :]
            base = ROW0 + 2 * (r - ROW0)
            held = []
            for j in range(joined):
                for c in range(2):
                    at = (1 + joined * i + j, pl.ds(base + c, 8, stride=2), slice(None))
                    held.append((at, s_ref[at] + e))
            for at, value in held:
                t_ref[at] = value

    loop(next_lv.planes, 8, plane)


def zero_margin(lv, ref):
    zero = jnp.zeros((8, LANES), F32)
    for y in (0, lv.planes + 1):
        for r in lv.tiles:
            ref[y, pl.ds(r, 8), :] = zero

    def plane(y):
        ref[y, pl.ds(0, 8), :] = zero
        ref[y, pl.ds(ROW0 + lv.n, 8), :] = zero

    loop(lv.planes + 2, 1, plane)


class Links:
    def __init__(self, send, recv):
        self.send, self.recv, self.used = send, recv, 0

    def group(self):
        index = self.used
        self.used += 1

        def copy(src, dst, device):
            return pltpu.make_async_remote_copy(
                src_ref=src,
                dst_ref=dst,
                send_sem=self.send.at[index],
                recv_sem=self.recv.at[index],
                device_id=device,
                device_id_type=MESH,
            )

        return copy


class Halo:
    def __init__(self, place, links, groups):
        gx, gy, nx, ny = place
        self.copies, self.waits = [], []
        for copies, whole in groups:
            copy = links.group()
            for (dx, dy), src, dst in copies:
                device = (lax.rem(gx + dx + nx, nx), lax.rem(gy + dy + ny, ny))
                self.copies.append(copy(src, dst, device))
            self.waits.append(copy(whole, whole, device))

    def start(self):
        for copy in self.copies:
            copy.start()

    def wait_recv(self):
        for wait in self.waits:
            wait.wait_recv()

    def wait_send(self):
        for wait in self.waits:
            wait.wait_send()


def there(place, dx, dy):
    gx, gy, nx, ny = place
    ok = None
    for at, by, size in ((gx, dx, nx), (gy, dy, ny)):
        if by:
            test = at + by < size if by > 0 else at + by >= 0
            ok = test if ok is None else jnp.logical_and(ok, test)
    return True if ok is None else ok


class Rim:
    def __init__(self, lv, halo, corner, refs):
        self.lv, self.halo, self.corner = lv, halo, corner
        self.send_x, self.send_y, self.recv_x, self.recv_y = refs

    @staticmethod
    def scratch(lv, halo, corner):
        n, parts = lv.n, lv.parts
        return [
            pltpu.VMEM((2, parts, halo, n, LANES), F32),
            pltpu.VMEM((2, parts, n, halo, LANES), F32),
            pltpu.VMEM((2, parts, halo, n, LANES), F32),
            pltpu.VMEM((2, parts, n + 2 * corner, halo, LANES), F32),
        ]

    def pack(self, ref):
        lv, h = self.lv, self.halo
        for side, start in ((0, lv.off), (1, lv.off + lv.n - h)):
            for p in range(lv.parts):
                for i in range(h):
                    self.send_x[side, p, i] = ref[p, start + i, pl.ds(ROW0, lv.n), :]

        def plane(i):
            for p in range(lv.parts):
                self.send_y[0, p, i] = ref[p, lv.off + i, pl.ds(ROW0, h), :]
                self.send_y[1, p, i] = ref[p, lv.off + i, pl.ds(ROW0 + lv.n - h, h), :]

        loop(lv.n, 2, plane)

    def exchange(self, place, links):
        c, n = self.corner, self.lv.n
        faces, others = [], []
        for dx, dy in NEIGHBOURS:
            if dy == 0:
                src = self.send_x.at[1 if dx > 0 else 0]
                faces.append(((dx, dy), src, self.recv_x.at[0 if dx > 0 else 1]))
                continue
            src = self.send_y.at[1 if dy > 0 else 0]
            dst = self.recv_y.at[0 if dy > 0 else 1]
            if dx == 0:
                dst = dst.at[:, c : c + n]
            elif dx > 0:
                src, dst = src.at[:, n - c : n], dst.at[:, 0:c]
            else:
                src, dst = src.at[:, 0:c], dst.at[:, c + n : n + 2 * c]
            others.append(((dx, dy), src, dst))
        return Halo(place, links, [(others, self.recv_y), (faces, self.recv_x)])

    def unpack(self, ref, place):
        lv, h, c, n = self.lv, self.halo, self.corner, self.lv.n
        for side, start, dx in ((0, lv.off - h, -1), (1, lv.off + n, 1)):
            ok = there(place, dx, 0)
            for p in range(lv.parts):
                for i in range(h):
                    value = self.recv_x[side, p, i]
                    ref[p, start + i, pl.ds(ROW0, n), :] = jnp.where(ok, value, 0.0)

        gx, gy, nx, ny = place

        def plane(i):
            cell = gx * n + (i - c)
            in_x = jnp.logical_and(cell >= 0, cell < nx * n)
            for side, row, dy in ((0, ROW0 - h, -1), (1, ROW0 + n, 1)):
                ok = jnp.logical_and(in_x, there(place, 0, dy))
                for p in range(lv.parts):
                    value = self.recv_y[side, p, i]
                    ref[p, lv.off - c + i, pl.ds(row, h), :] = jnp.where(ok, value, 0.0)

        loop(n + 2 * c, 2, plane)


class Blocks:
    def __init__(self, lv, refs):
        self.lv = lv
        self.send, self.recv = refs

    @staticmethod
    def scratch(lv):
        n = lv.n
        return [pltpu.VMEM((n, n, LANES), F32), pltpu.VMEM((8, n, n, LANES), F32)]

    def pack(self, ref):
        lv = self.lv
        for i in range(lv.n):
            self.send[i] = ref[0, lv.off + i, pl.ds(ROW0, lv.n), :]

    def exchange(self, place, links):
        n = self.lv.n
        copies = []
        for dx, dy in NEIGHBOURS:
            slot = (1 + dy) * 3 + 1 + dx
            slot -= 1 if slot > 4 else 0
            copies.append(((dx, dy), self.send, self.recv.at[slot]))
        return Halo(place, links, [(copies, self.recv)])

    def unpack(self, ref, place):
        lv, n = self.lv, self.lv.n
        for dx, dy in NEIGHBOURS:
            slot = (1 + dy) * 3 + 1 + dx
            slot -= 1 if slot > 4 else 0
            ok = there(place, -dx, -dy)
            for k in range(n):
                ref[0, lv.off - n * dx + k, pl.ds(ROW0 - n * dy, n), :] = jnp.where(
                    ok, self.recv[slot, k], 0.0
                )


class Gather:
    def __init__(self, place, links, piece_ref, whole_ref):
        gx, gy, nx, ny = place
        self.place = place
        self.piece, self.whole = piece_ref, whole_ref
        order_x = sorted(range(1, nx), key=lambda d: -min(d // 2, (nx - d) // 2))
        order_y = range(1, ny)
        mine = piece_ref.at[gx]
        copy = links.group()
        self.along_x = [copy(mine, mine, (lax.rem(gx + d, nx), gy)) for d in order_x]
        rest = piece_ref.at[0 : nx - 1]
        self.wait_x = copy(rest, rest, (lax.rem(gx + 1, nx), gy))
        slab = whole_ref.at[1 + gy, pl.ds(ROW0, 2 * nx), :]
        copy = links.group()
        self.along_y = [copy(slab, slab, (gx, lax.rem(gy + d, ny))) for d in order_y]
        rest = whole_ref.at[1:ny, pl.ds(ROW0, 2 * nx), :]
        self.wait_y = copy(rest, rest, (gx, lax.rem(gy + 1, ny)))

    def start_x(self, value):
        gx = self.place[0]
        self.piece[gx] = value
        for copy in self.along_x:
            copy.start()

    def start_y(self):
        gx, gy, nx, ny = self.place
        self.wait_x.wait_recv()
        for i in range(nx):
            self.whole[1 + gy, pl.ds(ROW0 + 2 * i, 2), :] = self.piece[i]
        for copy in self.along_y:
            copy.start()

    def finish(self):
        self.wait_y.wait_recv()

    def wait_send(self):
        self.wait_x.wait_send()
        self.wait_y.wait_send()


RIMS = {
    "rk0": (L0, 3, 2),
    "rb0": (L0, 2, 1),
    "rs0": (L0, 2, 1),
    "rk1": (L1, 7, 6),
    "rb1": (L1, 6, 5),
}


def scratch_shapes(nx, ny):
    l3, l4, l5 = coarse_levels(nx, ny)
    shapes = {}
    for name in ("raw_k", "raw_b"):
        shapes[name] = pltpu.VMEM((L0.n, L0.n, L0.parts * LANES), F32)
    shapes["perm"] = pltpu.VMEM((512, 512), BF16)
    shapes["left"] = pltpu.VMEM((8, 2 * LANES), F32)
    for i, lv in enumerate((L0, L1, L2)):
        for name in ("k", "b", "wx", "wy", "inv", "diag", "x", "s", "t"):
            shapes[name + str(i)] = pltpu.VMEM(lv.shape, F32)
        shapes["wz" + str(i)] = pltpu.VMEM((lv.parts + 1,) + lv.shape[1:], F32)
        shapes["tmp" + str(i)] = pltpu.VMEM((max(lv.parts // 2, 1), 8, 16, LANES), F32)
    shapes["e2"] = pltpu.VMEM((6, L2.rows, LANES), F32)
    for i, lv in ((3, l3), (4, l4), (5, l5)):
        for name in ("k", "b", "x", "s", "t"):
            shapes[name + str(i)] = pltpu.VMEM(lv.shape, F32)
        shapes["w" + str(i)] = pltpu.VMEM((8,) + lv.shape, F32)
    for name, (lv, halo, corner) in RIMS.items():
        for j, shape in enumerate(Rim.scratch(lv, halo, corner)):
            shapes[name + "_" + str(j)] = shape
    for name in ("rk2", "rb2", "rs2"):
        for j, shape in enumerate(Blocks.scratch(L2)):
            shapes[name + "_" + str(j)] = shape
    for name in ("pk3", "pb3"):
        shapes[name] = pltpu.VMEM((nx, 2, LANES), F32)
    copies = 5 * 2 + 3 + 2 * 2
    shapes["send"] = pltpu.SemaphoreType.DMA((copies,))
    shapes["recv"] = pltpu.SemaphoreType.DMA((copies,))
    shapes["local"] = pltpu.SemaphoreType.DMA((4,))
    return shapes


def coarse_levels(nx, ny):
    return (
        Coarse(ny, 2 * nx, 1, True),
        Coarse(ny, nx, 2, False),
        Coarse(ny // 2, nx // 2, 4, False),
    )


def kernel(nx, ny, names, b_in, k_in, out_ref, *refs):
    m = dict(zip(names, refs))
    gx, gy = lax.axis_index("gx"), lax.axis_index("gy")
    place = (gx, gy, nx, ny)
    l3, l4, l5 = coarse_levels(nx, ny)
    links = Links(m["send"], m["recv"])

    def pair(name, cls, *args):
        refs = [m[key] for key in names if key.startswith(name + "_")]
        return cls(*args, refs)

    rk0, rb0, rs0, rk1, rb1 = (pair(name, Rim, *RIMS[name]) for name in RIMS)
    rk2, rb2, rs2 = (pair(name, Blocks, L2) for name in ("rk2", "rb2", "rs2"))
    hk0, hb0, hs0, hk1, hb1, hk2, hb2, hs2 = (
        rim.exchange(place, links) for rim in (rk0, rb0, rs0, rk1, rb1, rk2, rb2, rs2)
    )
    gk3 = Gather(place, links, m["pk3"], m["k3"])
    gb3 = Gather(place, links, m["pb3"], m["b3"])

    load_k = pltpu.make_async_copy(k_in, m["raw_k"], m["local"].at[0])
    load_b = pltpu.make_async_copy(b_in, m["raw_b"], m["local"].at[1])
    load_k.start()
    load_b.start()

    barrier = pltpu.get_barrier_semaphore()
    peers = [(dx, dy) for dx, dy in NEIGHBOURS]
    peers += [(d, 0) for d in range(2, nx - 1)] + [(0, d) for d in range(2, ny - 1)]
    for dx, dy in peers:
        pl.semaphore_signal(
            barrier,
            inc=1,
            device_id=(lax.rem(gx + dx + nx, nx), lax.rem(gy + dy + ny, ny)),
            device_id_type=MESH,
        )

    def fill(i):
        start = pl.multiple_of(i * 64, 64)
        m["perm"][pl.ds(start, 64), :] = one(
            64, 512, lambda at, to: at + start == 4 * (to % LANES) + to // LANES
        )

    loop(8, 1, fill)
    m["left"][...] = jnp.zeros_like(m["left"])
    fold = one(
        2 * LANES,
        LANES,
        lambda at, to: jnp.logical_and(at // LANES == to // 64, (at % LANES) // 2 == to % 64),
    )
    unfold = one(
        LANES,
        2 * LANES,
        lambda at, to: jnp.logical_and(to // LANES == at // 64, (to % LANES) // 2 == at % 64),
    )

    def reorder(raw, ref):
        half = L0.n // 2
        for c in range(2):
            value = raw[c * half : (c + 1) * half].reshape(half * L0.n, 512)
            moved = exact_dot(value, m["perm"][...])
            for p in range(L0.parts):
                ref[p, pl.ds(L0.off + c * half, half), pl.ds(ROW0, L0.n), :] = moved[
                    :, p * LANES : (p + 1) * LANES
                ].reshape(half, L0.n, LANES)

    load_k.wait()
    reorder(m["raw_k"], m["k0"])
    rk0.pack(m["k0"])
    pl.semaphore_wait(barrier, len(peers))
    hk0.start()
    load_b.wait()
    reorder(m["raw_b"], m["b0"])
    rb0.pack(m["b0"])
    hb0.start()

    fold_x(L0, m["k0"], m["tmp0"])
    fold_y(L0, m["tmp0"], m["k1"], L1.off, 0.125)
    fold_x(L1, m["k1"], m["tmp1"])
    fold_y(L1, m["tmp1"], m["k2"], L2.off, 0.125)
    rk2.pack(m["k2"])
    hk2.start()
    fold_x(L2, m["k2"], m["tmp2"])
    gk3.start_x(fold_z(m["tmp2"], m["left"], fold, 0.125)[0:2])
    for lv, i in ((l3, 3), (l4, 4), (l5, 5)):
        for name in ("k", "x", "s", "t"):
            zero_margin(lv, m[name + str(i)])

    weights = [
        tuple(m[name + str(i)] for name in ("wx", "wy", "wz", "inv", "diag")) for i in range(3)
    ]
    sizes = [(nx * lv.n, ny * lv.n) for lv in (L0, L1, L2)]
    w3, w4, w5 = (m["w3"],), (m["w4"],), (m["w5"],)

    hk0.wait_recv()
    rk1.pack(m["k1"])
    hk1.start()
    rk0.unpack(m["k0"], place)
    fine_setup(L0, m["k0"], weights[0], gx, gy, *sizes[0])
    hb0.wait_recv()
    rb0.unpack(m["b0"], place)
    fine_first(L0, m["b0"], weights[0], m["x0"], 2)
    fine_step(L0, m["b0"], weights[0], m["x0"], None, m["s0"], 1, KEEP, OLD, STEP)
    fine_restrict(L0, m["b0"], weights[0], m["s0"], m["tmp0"])
    fold_y(L0, m["tmp0"], m["b1"], L1.off, 0.5)
    rb1.pack(m["b1"])
    hb1.start()
    rs0.pack(m["s0"])
    hs0.start()

    gk3.start_y()
    hk1.wait_recv()
    rk1.unpack(m["k1"], place)
    fine_setup(L1, m["k1"], weights[1], gx, gy, *sizes[1])
    hk2.wait_recv()
    rk2.unpack(m["k2"], place)
    fine_setup(L2, m["k2"], weights[2], gx, gy, *sizes[2])

    hb1.wait_recv()
    rb1.unpack(m["b1"], place)
    fine_first(L1, m["b1"], weights[1], m["x1"], 6)
    fine_step(L1, m["b1"], weights[1], m["x1"], None, m["s1"], 5, KEEP, OLD, STEP)
    fine_restrict(L1, m["b1"], weights[1], m["s1"], m["tmp1"], 4)
    fold_y(L1, m["tmp1"], m["b2"], L2.off, 0.5, 4)

    fine_first(L2, m["b2"], weights[2], m["x2"], 2)
    fine_step(L2, m["b2"], weights[2], m["x2"], None, m["s2"], 1, KEEP, OLD, STEP)
    fine_restrict(L2, m["b2"], weights[2], m["s2"], m["tmp2"])
    gb3.start_x(fold_z(m["tmp2"], m["left"], fold, 0.5)[0:2])
    rb2.pack(m["b2"])
    hb2.start()
    rs2.pack(m["s2"])
    hs2.start()

    gk3.finish()
    coarse_setup(l3, m["k3"], w3)
    gb3.start_y()
    coarse_fold(l3, l4, m["k3"], m["k4"], 0.125)
    coarse_setup(l4, m["k4"], w4)
    coarse_fold(l4, l5, m["k4"], m["k5"], 0.125)
    coarse_setup(l5, m["k5"], w5)
    for part in (hs0, hb2, hs2):
        part.wait_recv()
        part.wait_send()
    rs0.unpack(m["s0"], place)
    rb2.unpack(m["b2"], place)
    rs2.unpack(m["s2"], place)
    gb3.finish()

    coarse_first(l3, m["b3"], w3, m["x3"])
    coarse_step(l3, m["b3"], w3, m["x3"], None, m["s3"], KEEP, OLD, STEP)
    coarse_residual(l3, m["b3"], w3, m["s3"], m["t3"])
    coarse_fold(l3, l4, m["t3"], m["b4"], 0.5)
    coarse_first(l4, m["b4"], w4, m["x4"])
    coarse_step(l4, m["b4"], w4, m["x4"], None, m["s4"], KEEP, OLD, STEP)
    coarse_residual(l4, m["b4"], w4, m["s4"], m["t4"])
    coarse_fold(l4, l5, m["t4"], m["b5"], 0.5)
    coarse_first(l5, m["b5"], w5, m["x5"])
    now, old, spare = m["x5"], None, [m["s5"], m["t5"]]
    rho = RHO0
    for _ in range(COARSE_ITERS - 1):
        rho_new = 1.0 / (2.0 * SIGMA - rho)
        keep = 1.0 + rho_new * rho - 2.0 * rho_new / RADIUS
        out = spare.pop(0)
        coarse_step(l5, m["b5"], w5, now, old, out, keep, rho_new * rho, 2.0 * rho_new / RADIUS)
        if old is not None:
            spare.append(old)
        now, old, rho = out, now, rho_new
    coarse_correct(l4, l5, now, m["s4"], m["t4"])
    coarse_step(l4, m["b4"], w4, m["t4"], None, m["x4"], 1.0 - FIRST, 0.0, FIRST)
    coarse_step(l4, m["b4"], w4, m["x4"], m["t4"], m["s4"], KEEP, OLD, STEP)
    coarse_correct(l3, l4, m["s4"], m["s3"], m["t3"])
    coarse_step(l3, m["b3"], w3, m["t3"], None, m["x3"], 1.0 - FIRST, 0.0, FIRST)
    coarse_step(l3, m["b3"], w3, m["x3"], m["t3"], m["s3"], KEEP, OLD, STEP)

    near = jnp.concatenate(
        [m["s3"][gy + d, pl.ds(2 * gx + ROW0 - 2, 8), :] for d in range(3)], axis=0
    )
    wide = exact_dot(near, unfold)
    for d in range(3):
        for i in range(6):
            for a in range(2):
                row = wide[8 * d + i : 8 * d + i + 1, a * LANES : (a + 1) * LANES]
                m["e2"][i, pl.ds(ROW0 - 4 + 4 * d + 2 * a, 2), :] = jnp.broadcast_to(
                    row, (2, LANES)
                )
    for i in range(6):
        for k in range(2):
            x = L2.off - 4 + 2 * i + k
            for r in L2.tiles(4):
                m["t2"][0, x, pl.ds(r, 8), :] = (
                    m["s2"][0, x, pl.ds(r, 8), :] + m["e2"][i, pl.ds(r, 8), :]
                )
    fine_step(L2, m["b2"], weights[2], m["t2"], None, m["x2"], 3, 1.0 - FIRST, 0.0, FIRST)
    fine_step(L2, m["b2"], weights[2], m["x2"], m["t2"], m["s2"], 2, KEEP, OLD, STEP)

    fine_correct(L1, L2, m["s2"], m["s1"], m["t1"], 3)
    fine_step(L1, m["b1"], weights[1], m["t1"], None, m["x1"], 2, 1.0 - FIRST, 0.0, FIRST)
    fine_step(L1, m["b1"], weights[1], m["x1"], m["t1"], m["s1"], 1, KEEP, OLD, STEP)

    fine_correct(L0, L1, m["s1"], m["s0"], m["t0"], 2)
    fine_step(L0, m["b0"], weights[0], m["t0"], None, m["x0"], 1, 1.0 - FIRST, 0.0, FIRST)
    half = L0.n // 2
    stores = []
    for c in range(2):
        fine_step(
            L0, m["b0"], weights[0], m["x0"], m["t0"], m["s0"], 0, KEEP, OLD, STEP, c * half, half
        )
        stores.append(
            pltpu.make_async_copy(
                m["s0"].at[:, pl.ds(L0.off + c * half, half), pl.ds(ROW0, L0.n), :],
                out_ref.at[:, pl.ds(c * half, half)],
                m["local"].at[2 + c],
            )
        )
        stores[c].start()
    for part in (hk0, hb0, hk1, hb1, hk2, gk3, gb3):
        part.wait_send()
    for store in stores:
        store.wait()


CHUNKS = 1


def finish(parts_ref, out_ref, held, back, out, load_sem, store_sem):
    n = L0.n
    size = n // CHUNKS

    def chunk(c):
        return pl.ds(c * size, size)

    loads = [
        pltpu.make_async_copy(parts_ref.at[:, chunk(c)], held.at[:, chunk(c)], load_sem.at[c])
        for c in range(CHUNKS)
    ]
    stores = [
        pltpu.make_async_copy(out.at[chunk(c)], out_ref.at[chunk(c)], store_sem.at[c])
        for c in range(CHUNKS)
    ]
    for load in loads:
        load.start()

    def fill(i):
        start = pl.multiple_of(i * 64, 64)
        back[pl.ds(start, 64), :] = one(
            64, 512, lambda at, to: to == 4 * ((at + start) % LANES) + (at + start) // LANES
        )

    loop(8, 1, fill)
    for c in range(CHUNKS):
        loads[c].wait()
        value = jnp.concatenate(
            [held[p, chunk(c)].reshape(size * n, LANES) for p in range(L0.parts)], axis=1
        )
        out[chunk(c)] = exact_dot(value, back[...]).reshape(size, n, 512)
        stores[c].start()
    for store in stores:
        store.wait()


def solution(mesh):
    nx, ny = mesh.shape["gx"], mesh.shape["gy"]
    shapes = scratch_shapes(nx, ny)

    def body(right_side, coefficient):
        parts = pl.pallas_call(
            functools.partial(kernel, nx, ny, list(shapes)),
            out_shape=jax.ShapeDtypeStruct((L0.parts, L0.n, L0.n, LANES), F32),
            in_specs=[pl.BlockSpec(memory_space=pl.ANY)] * 2,
            out_specs=pl.BlockSpec(memory_space=pl.ANY),
            scratch_shapes=list(shapes.values()),
            compiler_params=pltpu.CompilerParams(
                collective_id=0, has_side_effects=True, vmem_limit_bytes=56 * 1024 * 1024
            ),
        )(right_side, coefficient)
        return pl.pallas_call(
            finish,
            out_shape=jax.ShapeDtypeStruct(right_side.shape, F32),
            in_specs=[pl.BlockSpec(memory_space=pl.ANY)],
            out_specs=pl.BlockSpec(memory_space=pl.ANY),
            scratch_shapes=[
                pltpu.VMEM((L0.parts, L0.n, L0.n, LANES), F32),
                pltpu.VMEM((512, 512), BF16),
                pltpu.VMEM((L0.n, L0.n, 512), F32),
                pltpu.SemaphoreType.DMA((CHUNKS,)),
                pltpu.SemaphoreType.DMA((CHUNKS,)),
            ],
            compiler_params=pltpu.CompilerParams(vmem_limit_bytes=60 * 1024 * 1024),
        )(parts)

    return jax.shard_map(
        body,
        mesh=mesh,
        in_specs=(P("gx", "gy", None), P("gx", "gy", None)),
        out_specs=P("gx", "gy", None),
        check_vma=False,
    )
```
